128 devices in a mesh: gauss: 16 (over y, z), view: 8 (over x, core).
Axes of the slice: x: 4, y: 4, z: 4, core: 2. Of those that a mesh axis runs over, the one named last changes fastest.
Arguments:
- table: bfloat16 [262144, 64], P(('gauss', 'view'))
- view_proj: float32 [8, 2, 4], P('view'), may hold values from -3 to 3
- lengths: int32 [8, 256], P('view', 'gauss'), may hold values from 1 to 1024, as said below
- lists: int32 [8, 256, 1024], P('view', 'gauss'), may hold values from 0 to 8191
- requests: int32 [8, 16, 128, 64], P('view', 'gauss'), may hold values from 0 to 2047
- target: bfloat16 [8, 256, 57, 256], P('view', 'gauss'), may hold values from -4 to 4
Outputs:
- image: float32 [8, 256, 57, 256], P('view', 'gauss')
- table_grad: float32 [262144, 64], P(('gauss', 'view'))
The draws below stay inside these ranges and needn't reach their ends.
Inputs may be any that keep to these rules, and one draw needn't show every extreme that they name: `lengths`: some tile of every view has all 1024 entries live.
All inputs are finite; a program needn't handle non-finite values.
Results may differ from the reference program's by a relative error of at most 0.0003.
Values may be sent and summed in bfloat16 or wider, within the bound.
No kernel may reach another device: no remote copies, remote signals or barrier semaphores. Data moves between devices by JAX's collectives and lax.ppermute only.
A program may use at most 64 MiB of HBM per device.

```python
import jax
import jax.numpy as jnp
from jax import lax

ROW_WIDTH = 64
FEATS = 57
GAUSS_DEV = 2048
CAP = 64
TILE_DEV = 16
MAXB = 4
V = 8
TILES = 256
NG = 262144
FETCH = 8192
N_GAUSS = 16
DEVICES = 128


def draw_table(key, part):
    keys = jax.random.split(key, 5)
    position = jax.random.normal(keys[0], (NG, 3), jnp.float32)
    scales = jax.random.uniform(keys[1], (NG, 2), jnp.float32, -3.0, -0.5)
    rotation = jax.random.normal(keys[2], (NG, 1), jnp.float32)
    opacity = jax.random.uniform(keys[3], (NG, 1), jnp.float32, -8.0, -1.0)
    features = 5.0 * jax.random.normal(keys[4], (NG, ROW_WIDTH - 7), jnp.float32)
    whole = jnp.concatenate([position, scales, rotation, opacity, features], axis=1)
    return whole.astype(jnp.bfloat16)


def draw_lengths(key, part):
    keys = jax.random.split(key, 4)
    most = MAXB * 256
    heavy = jax.random.randint(keys[0], (V, TILES // TILE_DEV, 1), 0, 4) == 0
    heavy = jnp.repeat(heavy.reshape(V, TILES // TILE_DEV), TILE_DEV, axis=1)
    light = jax.random.randint(keys[1], (V, TILES), 1, 3 * most // 4 + 1)
    big = jnp.minimum(jax.random.randint(keys[2], (V, TILES), 1, 2 * most + 1), most)
    extent = jnp.where(heavy, big, light)
    peak = jax.random.randint(keys[3], (V, 1), 0, TILES)
    column = jnp.arange(TILES, dtype=jnp.int32)[None, :]
    return jnp.where(column == peak, most, extent).astype(jnp.int32)


def touch_ends(values, stream_key, low, high):
    longest = values.shape.index(max(values.shape))
    spots = []
    for shift in (0, 1):
        where = [jax.random.randint(jax.random.fold_in(stream_key, axis), (), 0, length) for axis, length in enumerate(values.shape)]
        where[longest] = (where[longest] + shift) % values.shape[longest]
        spots.append(tuple(where))
    return values.at[spots[0]].set(low).at[spots[1]].set(high)


def shard_levels(own_key, dims, cuts, smallest, top_value):
    gain, own = 1.0, jax.random.fold_in(own_key, 6)
    for axis_at, blocks in cuts:
        heights = jnp.exp(jax.random.uniform(jax.random.fold_in(own, axis_at), (blocks,), jnp.float32, smallest / len(cuts), top_value / len(cuts)))
        gain = gain * jnp.repeat(heights, dims[axis_at] // blocks).reshape([-1 if axis == axis_at else 1 for axis in range(len(dims))])
    return gain


def bell_draw(key, shape, spread, most, shards=(), held_as=jnp.bfloat16):
    values = spread * jax.random.normal(key, shape, jnp.float32)
    if shards:
        values = values * shard_levels(key, shape, shards, -0.22, 0.18)
    return jnp.clip(values, -most, most).astype(held_as)


def setup_inputs(seed: int = 0) -> dict:
    arg_keys = jax.random.split(jax.random.key(seed), 7)
    return {
        "table": draw_table(jax.random.fold_in(arg_keys[6], 71), 0),
        "view_proj": bell_draw(arg_keys[1], (V, 2, 4), 0.6, 3.0, ((0, 8),), jnp.float32),
        "lengths": draw_lengths(jax.random.fold_in(arg_keys[6], 71), 0),
        "lists": touch_ends(jax.random.randint(arg_keys[3], (V, TILES, MAXB * 256), 0, FETCH), jax.random.fold_in(arg_keys[3], 1), 0, FETCH - 1).astype(jnp.int32),
        "requests": touch_ends(jax.random.randint(arg_keys[4], (V, N_GAUSS, DEVICES, CAP), 0, GAUSS_DEV), jax.random.fold_in(arg_keys[4], 1), 0, GAUSS_DEV - 1).astype(jnp.int32),
        "target": bell_draw(arg_keys[5], (V, TILES, FEATS, 256), 0.5, 4.0, ((0, 8), (1, 16))),
    }


def splat_block(splats, valid_mask, transmit, camera):
    pixel = jnp.arange(256, dtype=jnp.int32)
    pixel_x = (pixel % 16).astype(jnp.float32) + 0.5
    pixel_y = (pixel // 16).astype(jnp.float32) + 0.5
    proj_u = splats[:, 0] * camera[0, 0] + splats[:, 1] * camera[0, 1] + splats[:, 2] * camera[0, 2] + camera[0, 3]
    proj_w = splats[:, 0] * camera[1, 0] + splats[:, 1] * camera[1, 1] + splats[:, 2] * camera[1, 2] + camera[1, 3]
    center_u = 8.0 + 6.0 * jnp.tanh(proj_u)
    center_w = 8.0 + 6.0 * jnp.tanh(proj_w)
    coef_a = jnp.exp(splats[:, 3])
    coef_c = jnp.exp(splats[:, 4])
    coef_b = 0.9 * jnp.tanh(splats[:, 5]) * jnp.sqrt(coef_a * coef_c)
    opacity = jax.nn.sigmoid(splats[:, 6]) * valid_mask
    delta_u = pixel_x[:, None] - center_u[None, :]
    delta_w = pixel_y[:, None] - center_w[None, :]
    quad = coef_a[None, :] * delta_u * delta_u + 2.0 * coef_b[None, :] * delta_u * delta_w + coef_c[None, :] * delta_w * delta_w
    alpha = opacity[None, :] * jnp.exp(-0.5 * quad)
    logs = jnp.log1p(-alpha)
    inclusive = jnp.cumsum(logs, axis=1)
    weight = transmit[:, None] * jnp.exp(inclusive - logs) * alpha
    contrib = jnp.dot(splats[:, 7:].T, weight.T, precision=lax.Precision.HIGHEST, preferred_element_type=jnp.float32)
    return (contrib, transmit * jnp.exp(inclusive[:, -1]))

def render_tile(splats, extent, camera):
    entry = jnp.arange(splats.shape[0], dtype=jnp.int32)
    valid_mask = (entry < extent).astype(jnp.float32)
    transmit = jnp.ones((256,), jnp.float32)
    picture = jnp.zeros((splats.shape[1] - 7, 256), jnp.float32)
    for block_index in range(MAXB):
        lower = block_index * 256
        contrib, transmit = splat_block(splats[lower:lower + 256], valid_mask[lower:lower + 256], transmit, camera)
        picture = picture + contrib
    return picture

def reference(table, view_proj, lengths, lists, requests, target):
    owners = jnp.arange(DEVICES, dtype=jnp.int32)
    global_ids = (owners[None, None, :, None] * GAUSS_DEV + requests).reshape(V, N_GAUSS, CAP * DEVICES)

    def one_tile(grads, tile_index):
        view_index = tile_index // TILES
        local = tile_index % TILES
        ids = global_ids[view_index, local // TILE_DEV][lists[view_index, local]]
        splats = table[ids].astype(jnp.float32)
        camera = view_proj[view_index]
        extent = lengths[view_index, local]
        picture, pull = jax.vjp(lambda values: render_tile(values, extent, camera), splats)
        grow, = pull(picture - target[view_index, local].astype(jnp.float32))
        return (grads.at[ids].add(grow), picture)
    grads, pictures = lax.scan(one_tile, jnp.zeros((NG, ROW_WIDTH), jnp.float32), jnp.arange(V * TILES, dtype=jnp.int32))
    return (pictures.reshape(V, TILES, FEATS, 256), grads)
```

```python
import functools

import jax
import jax.numpy as jnp
from jax import lax
from jax.experimental import pallas as pl
from jax.experimental.pallas import tpu as pltpu
from jax.sharding import PartitionSpec as P

LOG2E = 1.4426950408889634
FEATS = 57
ROW = 64
LANE = 128
PIX = 256
GROUP = 32
ACCS = 4
UNROLL = 2
F32 = jnp.float32
BF16 = jnp.bfloat16


def split(x):
    hi = x.astype(BF16)
    lo = (x - hi.astype(F32)).astype(BF16)
    return hi, lo


def dot(a, b):
    return jnp.dot(a, b, preferred_element_type=F32)


def dot_t(a, b):
    return lax.dot_general(a, b, (((1,), (1,)), ((), ())), preferred_element_type=F32)


def unpack_rows(pairs_ref, rows_ref, peers):
    def step(i, c):
        for k in range(8):
            o = i * 8 + k
            two = pairs_ref[pl.ds(pl.multiple_of(o * 32, 32), 32), :].astype(F32)
            base = pl.multiple_of(o * 64, 64)
            rows_ref[pl.ds(base, 32), :] = two
            rows_ref[pl.ds(pl.multiple_of(base + 32, 32), 32), :] = pltpu.roll(two, 64, 1)
        return c

    lax.fori_loop(0, peers // 8, step, 0)


def pack_rows(accs, pairs_ref, peers):
    lane = lax.broadcasted_iota(jnp.int32, (32, LANE), 1)

    def step(i, c):
        for k in range(4):
            o = i * 4 + k
            base = pl.multiple_of(o * 64, 64)
            first = sum(acc[pl.ds(base, 32), :] for acc in accs)
            second = sum(acc[pl.ds(pl.multiple_of(base + 32, 32), 32), :] for acc in accs)
            pairs_ref[pl.ds(pl.multiple_of(o * 32, 32), 32), :] = jnp.where(
                lane < 64, first, pltpu.roll(second, 64, 1)
            )
        return c

    lax.fori_loop(0, peers // 4, step, 0)


def tiles_kernel(
    lens, lists, cam,
    pairs, target, prefix_mat, suffix_mat,
    image, out_pairs,
    rows, acc0, acc1, acc2, acc3, splats, grows, feat_t, par, geo, mom, weights, ratio, pic, tgt, grow_t,
):
    tiles = lens.shape[0]
    peers = pairs.shape[0] // 32
    accs = (acc0, acc1, acc2, acc3)
    entries = splats.shape[0]
    unpack_rows(pairs, rows, peers)

    def clear(i, c):
        for acc in accs:
            acc[pl.ds(pl.multiple_of(i * 64, 64), 64), :] = jnp.zeros((64, LANE), F32)
        return c

    lax.fori_loop(0, acc0.shape[0] // 64, clear, 0)
    tgt[...] = target[...].astype(F32)
    splats[...] = jnp.zeros_like(splats)
    feat_t[...] = jnp.zeros_like(feat_t)
    par[...] = jnp.zeros_like(par)
    mom[...] = jnp.zeros_like(mom)

    prefix = prefix_mat[...]
    suffix = suffix_mat[...]
    sub16 = lax.broadcasted_iota(jnp.int32, (16, LANE), 0).astype(F32) + 0.5

    def one_tile(t, carry):
        extent = lens[t]
        groups = (extent + GROUP - 1) // GROUP
        steps = (extent + UNROLL * LANE - 1) // (UNROLL * LANE)

        def gather(i, c):
            base = pl.multiple_of(i * GROUP, GROUP)
            got = [rows[pl.ds(lists[t * entries + base + j], 1), :] for j in range(GROUP)]
            for j in range(GROUP):
                splats[pl.ds(base + j, 1), :] = got[j]
            return c

        lax.fori_loop(0, groups, gather, 0)

        for b in range(8):
            @pl.when(b * LANE < extent)
            def _():
                turned = jnp.transpose(splats[b * LANE:(b + 1) * LANE, :])
                par[b * 8:(b + 1) * 8, :] = turned[56:64, :]
                feat_t[b] = turned[0:64, :].astype(BF16)

        entry = (
            lax.broadcasted_iota(jnp.int32, (8, LANE), 0) * LANE
            + lax.broadcasted_iota(jnp.int32, (8, LANE), 1)
        )

        def param(j):
            return jnp.where(entry < extent, par[pl.ds(j + 1, 8, stride=8), :], 0.0)

        px, py, pz = param(0), param(1), param(2)
        sa, sc, sb, so = param(3), param(4), param(5), param(6)
        tu = jnp.tanh(px * cam[0, 0] + py * cam[0, 1] + pz * cam[0, 2] + cam[0, 3])
        tw = jnp.tanh(px * cam[1, 0] + py * cam[1, 1] + pz * cam[1, 2] + cam[1, 3])
        ca, cc = jnp.exp(sa), jnp.exp(sc)
        tb = jnp.tanh(sb)
        root = 0.9 * jnp.sqrt(ca * cc)
        cb = tb * root
        soft = jnp.exp(-jnp.abs(so))
        log_o = jnp.minimum(so, 0.0) * LOG2E - jnp.log2(1.0 + soft)
        log_o = jnp.where(entry < extent, log_o, -1e30)
        rest = jnp.where(so >= 0.0, soft, 1.0) / (1.0 + soft)
        half = -0.5 * LOG2E
        geo[0] = 8.0 + 6.0 * tu
        geo[1] = 8.0 + 6.0 * tw
        geo[2] = half * ca
        geo[3] = (2.0 * half) * cb
        geo[4] = half * cc
        geo[5] = log_o

        pic[...] = jnp.zeros((64, PIX), F32)

        def coords(b):
            dx = sub16 - geo[0, pl.ds(b, 1), :]
            dy = sub16 - geo[1, pl.ds(b, 1), :]
            return dx, dy

        def forward(i, entering):
            for k in range(UNROLL):
                b = i * UNROLL + k
                dx, dy = coords(b)
                qa = geo[2, pl.ds(b, 1), :] * dx * dx
                qb = geo[3, pl.ds(b, 1), :] * dx
                qc = geo[4, pl.ds(b, 1), :] * dy * dy + geo[5, pl.ds(b, 1), :]
                power = qa[None] + qb[None] * dy[:, None, :] + qc[:, None, :]
                alpha = jnp.exp2(power.reshape(PIX, LANE))
                logs = jnp.log2(1.0 - alpha)
                ratio[b] = alpha * jnp.exp2(-logs)
                both = dot(jnp.concatenate(split(logs), axis=1), prefix)
                weight = alpha * jnp.exp2(both[:, :LANE] + entering)
                entering = entering + both[:, LANE:]
                halves = jnp.concatenate(split(weight), axis=1)
                weights[b] = halves
                ft = feat_t[b]
                pic[...] += dot_t(jnp.concatenate([ft, ft], axis=1), halves)
            return entering

        lax.fori_loop(0, steps, forward, jnp.zeros((PIX, LANE), F32))

        picture = pic[...]
        for h in range(2):
            image[h, pl.ds(t, FEATS, stride=tiles), :] = picture[:FEATS, h * LANE:(h + 1) * LANE]
        want = jnp.concatenate(
            [tgt[h, pl.ds(t, FEATS, stride=tiles), :] for h in range(2)], axis=1
        )
        want = jnp.concatenate([want, jnp.zeros((64 - FEATS, PIX), F32)], axis=0)
        feature = lax.broadcasted_iota(jnp.int32, (64, PIX), 0) < FEATS
        pull = jnp.where(feature, picture - want, 0.0)
        pull_hi, pull_lo = split(pull)
        pull_rows = jnp.concatenate([pull_hi, pull_lo], axis=0)
        pull_t = jnp.transpose(
            jnp.concatenate([pull_hi.astype(F32), pull_lo.astype(F32)], axis=0)
        ).astype(BF16)

        def backward(i, later):
            for k in range(UNROLL):
                b = (steps - 1 - i) * UNROLL + (UNROLL - 1 - k)
                dx, dy = coords(b)
                ft = feat_t[b]
                d_weight = dot(pull_t, jnp.concatenate([ft, ft], axis=0))
                halves = weights[b]
                weight = halves[:, :LANE].astype(F32) + halves[:, LANE:].astype(F32)
                prod = weight * d_weight
                both = dot(jnp.concatenate(split(prod), axis=1), suffix)
                h = prod - ratio[b] * (both[:, :LANE] + later)
                later = later + both[:, LANE:]
                h = h.reshape(16, 16, LANE)
                hy = h * dy[:, None, :]
                s0 = jnp.sum(h, axis=0)
                s1 = jnp.sum(hy, axis=0)
                s2 = jnp.sum(hy * dy[:, None, :], axis=0)
                sx = s0 * dx
                for j, m in enumerate((s0, sx, s1, sx * dx, s1 * dx, s2)):
                    mom[j, pl.ds(b, 1), :] = jnp.sum(m, axis=0, keepdims=True)
                quads = dot(pull_rows, halves)
                quads = quads[:64] + quads[64:]
                grow_t[b] = quads[:, :LANE] + quads[:, LANE:]
            return later

        lax.fori_loop(0, steps, backward, jnp.zeros((PIX, LANE), F32))

        m0, mx, my, mxx, mxy, myy = (mom[j] for j in range(6))
        du = (ca * mx + cb * my) * 6.0 * (1.0 - tu * tu)
        dw = (cb * mx + cc * my) * 6.0 * (1.0 - tw * tw)
        shared = -0.5 * cb * mxy
        outs = (
            du * cam[0, 0] + dw * cam[1, 0],
            du * cam[0, 1] + dw * cam[1, 1],
            du * cam[0, 2] + dw * cam[1, 2],
            -0.5 * ca * mxx + shared,
            -0.5 * cc * myy + shared,
            -mxy * root * (1.0 - tb * tb),
            rest * m0,
        )
        for j, value in enumerate(outs):
            par[pl.ds(j + 1, 8, stride=8), :] = value
        keep = lax.broadcasted_iota(jnp.int32, (8, LANE), 0) == 0

        for b in range(8):
            @pl.when(b * LANE < extent)
            def _():
                last = jnp.where(keep, grow_t[b, 56:64, :], par[b * 8:(b + 1) * 8, :])
                whole = jnp.concatenate([grow_t[b, 0:56, :], last, jnp.zeros((64, LANE), F32)], axis=0)
                grows[b * LANE:(b + 1) * LANE, :] = jnp.transpose(whole)

        def scatter(i, c):
            base = pl.multiple_of(i * GROUP, GROUP)
            block = [grows[pl.ds(base + j, 1), :] for j in range(GROUP)]
            ids = [lists[t * entries + base + j] for j in range(GROUP)]

            for j in range(0, GROUP, ACCS):
                old = [accs[k][pl.ds(ids[j + k], 1), :] for k in range(ACCS)]
                for k in range(ACCS):
                    accs[k][pl.ds(ids[j + k], 1), :] = old[k] + block[j + k]
            return c

        lax.fori_loop(0, groups, scatter, 0)
        return carry

    lax.fori_loop(0, tiles, one_tile, 0)
    pack_rows(accs, out_pairs, peers)


def triangles():
    r = lax.broadcasted_iota(jnp.int32, (PIX, PIX), 0) % LANE
    c = lax.broadcasted_iota(jnp.int32, (PIX, PIX), 1)
    prefix = (c >= LANE) | (r < c)
    suffix = (c >= LANE) | (r > c)
    return prefix.astype(BF16), suffix.astype(BF16)


def render(lens, lists, cam, pairs, target):
    tiles, entries = lists.shape
    peers = pairs.shape[0] // 32
    smem = pl.BlockSpec(memory_space=pltpu.SMEM)
    vmem = pl.BlockSpec(memory_space=pltpu.VMEM)
    prefix, suffix = triangles()
    t2 = jnp.transpose(target, (1, 0, 2)).reshape(FEATS * tiles, PIX)
    t2 = jnp.stack([t2[:, :LANE], t2[:, LANE:]])
    image, grads = pl.pallas_call(
        tiles_kernel,
        out_shape=(
            jax.ShapeDtypeStruct((2, FEATS * tiles, LANE), F32),
            jax.ShapeDtypeStruct((peers * 32, LANE), F32),
        ),
        in_specs=[smem] * 3 + [vmem] * 4,
        out_specs=(vmem, vmem),
        scratch_shapes=[
            *[pltpu.VMEM((peers * 64, LANE), F32)] * (1 + ACCS),
            pltpu.VMEM((entries, LANE), F32),
            pltpu.VMEM((entries, LANE), F32),
            pltpu.VMEM((8, ROW, LANE), BF16),
            pltpu.VMEM((64, LANE), F32),
            pltpu.VMEM((6, 8, LANE), F32),
            pltpu.VMEM((6, 8, LANE), F32),
            pltpu.VMEM((8, PIX, 2 * LANE), BF16),
            pltpu.VMEM((8, PIX, LANE), F32),
            pltpu.VMEM((64, PIX), F32),
            pltpu.VMEM((2, FEATS * tiles, LANE), F32),
            pltpu.VMEM((8, ROW, LANE), F32),
        ],
        compiler_params=pltpu.CompilerParams(vmem_limit_bytes=48 << 20),
    )(lens, lists.reshape(-1), cam, pairs, t2, prefix, suffix)
    image = jnp.concatenate([image[0], image[1]], axis=1).reshape(FEATS, tiles, PIX)
    return jnp.transpose(image, (1, 0, 2)), grads


def serve_kernel(slot_major, table_lo, served):
    peers = slot_major.shape[1]
    lane = lax.broadcasted_iota(jnp.int32, (64, LANE), 1)
    upper = lane // 64
    mat = table_lo[...]

    def step(g, c):
        ids = pltpu.roll(slot_major[...], lax.rem(peers - g * 8, peers), 1)
        for k in range(8):
            col = jnp.broadcast_to(ids[:, k:k + 1], (64, LANE))
            low = col & 255
            high = (col >> 8) - upper
            hot = [jnp.where(low == lane + q * LANE, 1.0, 0.0).astype(BF16) for q in range(2)]
            got = dot_t(jnp.concatenate(hot, axis=1), mat)
            total = jnp.zeros((64, LANE), F32)
            for q in range(4):
                total = total + jnp.where(high == 2 * q, got[:, q * LANE:(q + 1) * LANE], 0.0)
            total = total + pltpu.roll(total, 64, 1)
            out = jnp.where(lane[:32] < 64, total[:32], total[32:])
            served[pl.ds(pl.multiple_of((g * 8 + k) * 32, 32), 32), :] = out.astype(BF16)
        return c

    lax.fori_loop(0, peers // 8, step, 0)


def serve(incoming, table):
    peers = incoming.shape[0]
    turned = jnp.transpose(table)
    turned = jnp.concatenate([turned[ROW - FEATS:], turned[:ROW - FEATS]], axis=0)
    turned = turned.reshape(ROW, 8, PIX).transpose(1, 0, 2).reshape(8 * ROW, PIX)
    vmem = pl.BlockSpec(memory_space=pltpu.VMEM)
    return pl.pallas_call(
        serve_kernel,
        out_shape=jax.ShapeDtypeStruct((peers * 32, LANE), BF16),
        in_specs=[vmem, vmem],
        out_specs=vmem,
        compiler_params=pltpu.CompilerParams(vmem_limit_bytes=32 << 20),
    )(jnp.transpose(incoming), turned)


def collect_kernel(slot_major, flat, pairs, owned, total):
    peers = slot_major.shape[1]
    lane = lax.broadcasted_iota(jnp.int32, (64, LANE), 1)
    upper = lane // 64
    left = lane[:32] < 64
    low_id = lax.broadcasted_iota(jnp.int32, (512, LANE), 0)
    total[...] = jnp.zeros_like(total)

    def step(g, c):
        ids = pltpu.roll(slot_major[...], lax.rem(peers - g * 8, peers), 1)
        hot = []
        for k in range(4):
            row = flat[pl.ds(g * 4 + k, 1), :] & 511
            hot.append(jnp.where(low_id == row, 1.0, 0.0).astype(BF16))
        blocks = []
        for k in range(8):
            high = (jnp.broadcast_to(ids[:, k:k + 1], (64, LANE)) >> 9) - upper
            two = pairs[pl.ds(pl.multiple_of((g * 8 + k) * 32, 32), 32), :]
            other = pltpu.roll(two, 64, 1)
            both = jnp.concatenate(
                [jnp.where(left, two, other), jnp.where(left, other, two)], axis=0
            )
            hi = both.astype(BF16).astype(F32)
            parts = [
                jnp.where(high == 2 * q, part, 0.0).astype(BF16)
                for part in (hi, both - hi)
                for q in range(2)
            ]
            blocks.append(jnp.concatenate(parts, axis=1))
        total[...] += dot(jnp.concatenate(hot, axis=1), jnp.concatenate(blocks, axis=0))
        return c

    lax.fori_loop(0, peers // 8, step, 0)
    whole = jnp.transpose(total[:, :256] + total[:, 256:])
    for q in range(4):
        part = whole[q * 64:(q + 1) * 64]
        owned[:, q * 512:(q + 1) * 512] = jnp.concatenate([part[FEATS:], part[:FEATS]], axis=0)


def collect(incoming, pairs, rows):
    peers = incoming.shape[0]
    vmem = pl.BlockSpec(memory_space=pltpu.VMEM)
    owned = pl.pallas_call(
        collect_kernel,
        out_shape=jax.ShapeDtypeStruct((ROW, rows), F32),
        in_specs=[vmem] * 3,
        out_specs=vmem,
        scratch_shapes=[pltpu.VMEM((512, 512), F32)],
        compiler_params=pltpu.CompilerParams(vmem_limit_bytes=32 << 20),
    )(jnp.transpose(incoming), incoming.reshape(-1, LANE), pairs)
    return jnp.transpose(owned)


def exchange(x):
    return lax.all_to_all(x, ("gauss", "view"), split_axis=0, concat_axis=0, tiled=True)


def shards(table, view_proj, lengths, lists, requests, target):
    incoming = exchange(requests[0, 0])
    peers = incoming.shape[0]
    served = serve(incoming, table)
    pairs = exchange(served.reshape(peers, 32, LANE)).reshape(peers * 32, LANE)
    image, grads = render(lengths[0], lists[0], view_proj[0], pairs, target[0])
    returned = exchange(grads.reshape(peers, 32, LANE)).reshape(peers * 32, LANE)
    return image[None], collect(incoming, returned, table.shape[0])


def solution(mesh):
    return jax.shard_map(
        shards,
        mesh=mesh,
        in_specs=(
            P(("gauss", "view"), None),
            P("view", None, None),
            P("view", "gauss"),
            P("view", "gauss", None),
            P("view", "gauss", None, None),
            P("view", "gauss", None, None),
        ),
        out_specs=(P("view", "gauss", None, None), P(("gauss", "view"), None)),
        check_vma=False,
    )
```

```python
import functools

import jax
import jax.numpy as jnp
from jax import lax
from jax.experimental import pallas as pl
from jax.experimental.pallas import tpu as pltpu
from jax.sharding import PartitionSpec as P

LOG2E = 1.4426950408889634
FEATS = 57
ROW = 64
LANE = 128
PIX = 256
ACCS = 4
STEP = 256
RING = 9
PAD = 16
F32 = jnp.float32
BF16 = jnp.bfloat16


def split(x):
    hi = x.astype(BF16)
    lo = (x - hi.astype(F32)).astype(BF16)
    return hi, lo


def dot(a, b):
    return jnp.dot(a, b, preferred_element_type=F32)


def dot_t(a, b):
    return lax.dot_general(a, b, (((1,), (1,)), ((), ())), preferred_element_type=F32)


def unpack_rows(pairs_ref, rows_ref, peers):
    def step(i, c):
        for k in range(8):
            o = i * 8 + k
            two = pairs_ref[pl.ds(pl.multiple_of(o * 32, 32), 32), :].astype(F32)
            base = pl.multiple_of(o * 64, 64)
            rows_ref[pl.ds(base, 32), :] = two
            rows_ref[pl.ds(pl.multiple_of(base + 32, 32), 32), :] = pltpu.roll(two, 64, 1)
        return c

    lax.fori_loop(0, peers // 8, step, 0)


def pack_rows(accs, pairs_ref, peers):
    lane = lax.broadcasted_iota(jnp.int32, (32, LANE), 1)

    def step(i, c):
        for k in range(4):
            o = i * 4 + k
            base = pl.multiple_of(o * 64, 64)
            first = sum(acc[pl.ds(base, 32), :] for acc in accs)
            second = sum(acc[pl.ds(pl.multiple_of(base + 32, 32), 32), :] for acc in accs)
            pairs_ref[pl.ds(pl.multiple_of(o * 32, 32), 32), :] = jnp.where(
                lane < 64, first, pltpu.roll(second, 64, 1)
            )
        return c

    lax.fori_loop(0, peers // 4, step, 0)


def tiles_kernel(
    lens, lists, cam,
    pairs, target, prefix_mat, suffix_mat,
    image, out_pairs,
    base_of, tile_of, first_of, mirror_of, live_of,
    rows, acc0, acc1, acc2, acc3,
    splats, grows, feat_t, geo, weights, ratio, entering_ref, later_ref, pic, tgt, pull_rows, pull_t, grow_t,
):
    accs = (acc0, acc1, acc2, acc3)
    tiles = lens.shape[0]
    peers = pairs.shape[0] // 32
    entries = lists.shape[0] // (tiles + 1)

    def blank(i, c):
        base_of[i] = tiles * entries
        tile_of[i] = 0
        first_of[i] = 1
        mirror_of[i] = 0
        live_of[i] = 0
        return c

    lax.fori_loop(0, base_of.shape[0], blank, 0)

    def list_tile(t, at):
        steps = (lens[t] + STEP - 1) // STEP

        def list_step(j, c):
            where = at + j + PAD
            base_of[where] = t * entries + j * STEP
            tile_of[where] = t
            first_of[where] = jnp.where(j == 0, 1, 0)
            mirror_of[where] = at + steps - 1 - j
            live_of[where] = lens[t] - j * STEP
            return c

        lax.fori_loop(0, steps, list_step, 0)
        return at + steps

    count = lax.fori_loop(0, tiles, list_tile, 0)

    unpack_rows(pairs, rows, peers)
    rows[peers * 64:, :] = jnp.zeros((8, LANE), F32)

    def clear(i, c):
        for acc in accs:
            acc[pl.ds(pl.multiple_of(i * 64, 64), 64), :] = jnp.zeros((64, LANE), F32)
        return c

    lax.fori_loop(0, peers, clear, 0)
    tgt[...] = target[...].astype(F32)
    splats[...] = jnp.zeros_like(splats)
    feat_t[0:2] = jnp.zeros((2, ROW, STEP), BF16)
    geo[0:2] = jnp.zeros((2, 16, STEP), F32)

    prefix = prefix_mat[...]
    suffix = suffix_mat[...]
    sub16 = lax.broadcasted_iota(jnp.int32, (16, STEP), 0).astype(F32) + 0.5
    lane256 = lax.broadcasted_iota(jnp.int32, (1, STEP), 1)
    feature = lax.broadcasted_iota(jnp.int32, (64, PIX), 0) < FEATS

    def scatter(s):
        base = base_of[mirror_of[s + PAD] + PAD]
        base = jnp.where(live_of[s + PAD] > 0, base, tiles * entries)
        for q in range(0, STEP, ACCS):
            ids = [lists[base + q + k] for k in range(ACCS)]
            old = [accs[k][pl.ds(ids[k], 1), :] for k in range(ACCS)]
            for k in range(ACCS):
                accs[k][pl.ds(ids[k], 1), :] = old[k] + grows[q + k:q + k + 1, :]

    def turn_back():
        for k in range(2):
            part = jnp.concatenate(
                [grow_t[:, k * LANE:(k + 1) * LANE], jnp.zeros((64, LANE), F32)], axis=0
            )
            grows[k * LANE:(k + 1) * LANE, :] = jnp.transpose(part)

    def coords(g):
        return sub16 - geo[g, 0:1, :], sub16 - geo[g, 1:2, :]

    def backward(b):
        f = mirror_of[b + PAD]
        g = f + 2
        slot = lax.rem(g, RING)
        t = tile_of[b + PAD]
        keep = first_of[b + PAD] == 0
        dx, dy = coords(g)
        ft = feat_t[g]
        halves = weights[slot]
        d_weight = dot(pull_t[t], jnp.concatenate([ft, ft], axis=0))
        quads = dot(pull_rows[t], halves)
        quads = quads[:64] + quads[64:]
        later = jnp.where(keep, later_ref[...], 0.0)
        sums = [None, None]
        for k in (1, 0):
            cut = slice(k * LANE, (k + 1) * LANE)
            weight = (
                halves[:, 2 * k * LANE:(2 * k + 1) * LANE].astype(F32)
                + halves[:, (2 * k + 1) * LANE:(2 * k + 2) * LANE].astype(F32)
            )
            prod = weight * d_weight[:, cut]
            both = dot(jnp.concatenate(split(prod), axis=1), suffix)
            h = prod - ratio[slot, :, cut] * (both[:, :LANE] + later)
            later = later + both[:, LANE:]
            h = h.reshape(16, 16, LANE)
            dyk = dy[:, cut]
            hy = h * dyk[:, None, :]
            sums[k] = (
                jnp.sum(h, axis=0),
                jnp.sum(hy, axis=0),
                jnp.sum(hy * dyk[:, None, :], axis=0),
            )
        later_ref[...] = later
        s0, s1, s2 = (jnp.concatenate([sums[0][j], sums[1][j]], axis=1) for j in range(3))
        sx = s0 * dx
        m0, mx, my, mxx, mxy, myy = (
            jnp.sum(m, axis=0, keepdims=True) for m in (s0, sx, s1, sx * dx, s1 * dx, s2)
        )
        ca, cb, cc = geo[g, 6:7, :], geo[g, 7:8, :], geo[g, 8:9, :]
        du = (ca * mx + cb * my) * geo[g, 9:10, :]
        dw = (cb * mx + cc * my) * geo[g, 10:11, :]
        shared = -0.5 * cb * mxy
        first = jnp.concatenate(
            [quads[:, 0:LANE] + quads[:, LANE:2 * LANE],
             quads[:, 2 * LANE:3 * LANE] + quads[:, 3 * LANE:]], axis=1
        )
        grow_t[0:56, :] = first[0:56]
        grow_t[56:57, :] = first[56:57]
        outs = (
            du * cam[0, 0] + dw * cam[1, 0],
            du * cam[0, 1] + dw * cam[1, 1],
            du * cam[0, 2] + dw * cam[1, 2],
            -0.5 * ca * mxx + shared,
            -0.5 * cc * myy + shared,
            -mxy * geo[g, 11:12, :],
            geo[g, 12:13, :] * m0,
        )
        for j, value in enumerate(outs):
            grow_t[57 + j:58 + j, :] = value

    def pull(p):
        t = tile_of[p + PAD]
        picture = pic[...]
        for h in range(2):
            image[h, pl.ds(t, FEATS, stride=tiles), :] = picture[:FEATS, h * LANE:(h + 1) * LANE]
        want = jnp.concatenate(
            [tgt[h, pl.ds(t, FEATS, stride=tiles), :] for h in range(2)], axis=1
        )
        want = jnp.concatenate([want, jnp.zeros((64 - FEATS, PIX), F32)], axis=0)
        diff = jnp.where(feature, picture - want, 0.0)
        hi, lo = split(diff)
        both = jnp.concatenate([hi, lo], axis=0)
        pull_rows[t] = both
        pull_t[t] = jnp.transpose(both.astype(F32)).astype(BF16)

    def forward(f):
        g = f + 2
        slot = lax.rem(g, RING)
        keep = first_of[f + PAD] == 0
        dx, dy = coords(g)
        qa = geo[g, 2:3, :] * dx * dx
        qb = geo[g, 3:4, :] * dx
        qc = geo[g, 4:5, :] * dy * dy + geo[g, 5:6, :]
        entering = jnp.where(keep, entering_ref[...], 0.0)
        parts = []
        for k in range(2):
            cut = slice(k * LANE, (k + 1) * LANE)
            power = qa[None, :, cut] + qb[None, :, cut] * dy[:, None, cut] + qc[:, None, cut]
            alpha = jnp.exp2(power.reshape(PIX, LANE))
            logs = jnp.log2(1.0 - alpha)
            both = dot(jnp.concatenate(split(logs), axis=1), prefix)
            weight = alpha * jnp.exp2(both[:, :LANE] + entering)
            entering = entering + both[:, LANE:]
            ratio[slot, :, cut] = alpha * jnp.exp2(-logs)
            parts.extend(split(weight))
        entering_ref[...] = entering
        halves = jnp.concatenate(parts, axis=1)
        weights[slot] = halves
        ft = feat_t[g]
        left, right = ft[:, :LANE], ft[:, LANE:]
        pic[...] = jnp.where(keep, pic[...], 0.0) + dot_t(
            jnp.concatenate([left, left, right, right], axis=1), halves
        )

    def prepare(x):
        g = x + 2
        turned = [
            jnp.transpose(splats[k * LANE:(k + 1) * LANE, :])[0:64] for k in range(2)
        ]
        turned = jnp.concatenate(turned, axis=1)
        feat_t[g] = turned.astype(BF16)
        px, py, pz, sa, sc, sb, so = (turned[57 + j:58 + j, :] for j in range(7))
        tu = jnp.tanh(px * cam[0, 0] + py * cam[0, 1] + pz * cam[0, 2] + cam[0, 3])
        tw = jnp.tanh(px * cam[1, 0] + py * cam[1, 1] + pz * cam[1, 2] + cam[1, 3])
        ca, cc = jnp.exp(sa), jnp.exp(sc)
        tb = jnp.tanh(sb)
        root = 0.9 * jnp.sqrt(ca * cc)
        cb = tb * root
        soft = jnp.exp(-jnp.abs(so))
        log_o = jnp.minimum(so, 0.0) * LOG2E - jnp.log2(1.0 + soft)
        half = -0.5 * LOG2E
        values = (
            8.0 + 6.0 * tu,
            8.0 + 6.0 * tw,
            half * ca,
            (2.0 * half) * cb,
            half * cc,
            jnp.where(lane256 < live_of[x + PAD], log_o, -1e30),
            ca,
            cb,
            cc,
            6.0 * (1.0 - tu * tu),
            6.0 * (1.0 - tw * tw),
            root * (1.0 - tb * tb),
            jnp.where(so >= 0.0, soft, 1.0) / (1.0 + soft),
        )
        for j, value in enumerate(values):
            geo[g, j:j + 1, :] = value

    def gather(n):
        base = base_of[n + PAD]
        for q in range(0, STEP, 32):
            got = [rows[pl.ds(lists[base + q + j], 1), :] for j in range(32)]
            for j in range(32):
                splats[q + j:q + j + 1, :] = got[j]

    def opening(n, c):
        pull(n - 3)
        forward(n - 2)
        prepare(n - 1)
        gather(n)
        return c

    def middle(n, c):
        scatter(n - 9)
        turn_back()
        backward(n - 7)
        pull(n - 3)
        forward(n - 2)
        prepare(n - 1)
        gather(n)
        return c

    def closing(n, c):
        scatter(n - 9)
        turn_back()
        backward(n - 7)
        return c

    lax.fori_loop(0, 7, opening, 0)
    lax.fori_loop(7, count + 3, middle, 0)
    lax.fori_loop(count + 3, count + 9, closing, 0)
    pack_rows(accs, out_pairs, peers)


def triangles():
    r = lax.broadcasted_iota(jnp.int32, (PIX, PIX), 0) % LANE
    c = lax.broadcasted_iota(jnp.int32, (PIX, PIX), 1)
    prefix = (c >= LANE) | (r < c)
    suffix = (c >= LANE) | (r > c)
    return prefix.astype(BF16), suffix.astype(BF16)


def render(lens, lists, cam, pairs, target):
    tiles, entries = lists.shape
    peers = pairs.shape[0] // 32
    steps = tiles * (entries // STEP)
    live = lax.broadcasted_iota(jnp.int32, lists.shape, 1) < lens[:, None]
    flat = jnp.where(live, lists, peers * 64).reshape(-1)
    flat = jnp.concatenate([flat, jnp.full((entries,), peers * 64, jnp.int32)])
    smem = pl.BlockSpec(memory_space=pltpu.SMEM)
    vmem = pl.BlockSpec(memory_space=pltpu.VMEM)
    prefix, suffix = triangles()
    t2 = jnp.transpose(target, (1, 0, 2)).reshape(FEATS * tiles, PIX)
    t2 = jnp.stack([t2[:, :LANE], t2[:, LANE:]])
    image, grads = pl.pallas_call(
        tiles_kernel,
        out_shape=(
            jax.ShapeDtypeStruct((2, FEATS * tiles, LANE), F32),
            jax.ShapeDtypeStruct((peers * 32, LANE), F32),
        ),
        in_specs=[smem] * 3 + [vmem] * 4,
        out_specs=(vmem, vmem),
        scratch_shapes=[
            *[pltpu.SMEM((steps + 2 * PAD,), jnp.int32)] * 5,
            *[pltpu.VMEM((peers * 64 + 8, LANE), F32)] * (1 + ACCS),
            pltpu.VMEM((STEP, LANE), F32),
            pltpu.VMEM((STEP, LANE), F32),
            pltpu.VMEM((steps + 4, ROW, STEP), BF16),
            pltpu.VMEM((steps + 4, 16, STEP), F32),
            pltpu.VMEM((RING, PIX, 2 * STEP), BF16),
            pltpu.VMEM((RING, PIX, STEP), F32),
            pltpu.VMEM((PIX, LANE), F32),
            pltpu.VMEM((PIX, LANE), F32),
            pltpu.VMEM((64, PIX), F32),
            pltpu.VMEM((2, FEATS * tiles, LANE), F32),
            pltpu.VMEM((tiles, 2 * ROW, PIX), BF16),
            pltpu.VMEM((tiles, PIX, 2 * ROW), BF16),
            pltpu.VMEM((ROW, STEP), F32),
        ],
        compiler_params=pltpu.CompilerParams(vmem_limit_bytes=52 << 20),
    )(lens, flat, cam, pairs, t2, prefix, suffix)
    image = jnp.concatenate([image[0], image[1]], axis=1).reshape(FEATS, tiles, PIX)
    return jnp.transpose(image, (1, 0, 2)), grads


def serve_kernel(slot_major, table_lo, served):
    peers = slot_major.shape[1]
    lane = lax.broadcasted_iota(jnp.int32, (64, LANE), 1)
    upper = lane // 64
    mat = table_lo[...]

    def step(g, c):
        ids = pltpu.roll(slot_major[...], lax.rem(peers - g * 8, peers), 1)
        for k in range(8):
            col = jnp.broadcast_to(ids[:, k:k + 1], (64, LANE))
            low = col & 255
            high = (col >> 8) - upper
            hot = [jnp.where(low == lane + q * LANE, 1.0, 0.0).astype(BF16) for q in range(2)]
            got = dot_t(jnp.concatenate(hot, axis=1), mat)
            total = jnp.zeros((64, LANE), F32)
            for q in range(4):
                total = total + jnp.where(high == 2 * q, got[:, q * LANE:(q + 1) * LANE], 0.0)
            total = total + pltpu.roll(total, 64, 1)
            out = jnp.where(lane[:32] < 64, total[:32], total[32:])
            served[pl.ds(pl.multiple_of((g * 8 + k) * 32, 32), 32), :] = out.astype(BF16)
        return c

    lax.fori_loop(0, peers // 8, step, 0)


def serve(incoming, table):
    peers = incoming.shape[0]
    turned = jnp.transpose(table)
    turned = jnp.concatenate([turned[ROW - FEATS:], turned[:ROW - FEATS]], axis=0)
    turned = turned.reshape(ROW, 8, PIX).transpose(1, 0, 2).reshape(8 * ROW, PIX)
    vmem = pl.BlockSpec(memory_space=pltpu.VMEM)
    return pl.pallas_call(
        serve_kernel,
        out_shape=jax.ShapeDtypeStruct((peers * 32, LANE), BF16),
        in_specs=[vmem, vmem],
        out_specs=vmem,
        compiler_params=pltpu.CompilerParams(vmem_limit_bytes=32 << 20),
    )(jnp.transpose(incoming), turned)


def collect_kernel(slot_major, flat, pairs, owned, total):
    peers = slot_major.shape[1]
    lane = lax.broadcasted_iota(jnp.int32, (64, LANE), 1)
    upper = lane // 64
    left = lane[:32] < 64
    low_id = lax.broadcasted_iota(jnp.int32, (512, LANE), 0)
    total[...] = jnp.zeros_like(total)

    def step(g, c):
        ids = pltpu.roll(slot_major[...], lax.rem(peers - g * 8, peers), 1)
        hot = []
        for k in range(4):
            row = flat[pl.ds(g * 4 + k, 1), :] & 511
            hot.append(jnp.where(low_id == row, 1.0, 0.0).astype(BF16))
        blocks = []
        for k in range(8):
            high = (jnp.broadcast_to(ids[:, k:k + 1], (64, LANE)) >> 9) - upper
            two = pairs[pl.ds(pl.multiple_of((g * 8 + k) * 32, 32), 32), :]
            other = pltpu.roll(two, 64, 1)
            both = jnp.concatenate(
                [jnp.where(left, two, other), jnp.where(left, other, two)], axis=0
            )
            hi = both.astype(BF16).astype(F32)
            parts = [
                jnp.where(high == 2 * q, part, 0.0).astype(BF16)
                for part in (hi, both - hi)
                for q in range(2)
            ]
            blocks.append(jnp.concatenate(parts, axis=1))
        total[...] += dot(jnp.concatenate(hot, axis=1), jnp.concatenate(blocks, axis=0))
        return c

    lax.fori_loop(0, peers // 8, step, 0)
    whole = jnp.transpose(total[:, :256] + total[:, 256:])
    for q in range(4):
        part = whole[q * 64:(q + 1) * 64]
        owned[:, q * 512:(q + 1) * 512] = jnp.concatenate([part[FEATS:], part[:FEATS]], axis=0)


def collect(incoming, pairs, rows):
    peers = incoming.shape[0]
    vmem = pl.BlockSpec(memory_space=pltpu.VMEM)
    owned = pl.pallas_call(
        collect_kernel,
        out_shape=jax.ShapeDtypeStruct((ROW, rows), F32),
        in_specs=[vmem] * 3,
        out_specs=vmem,
        scratch_shapes=[pltpu.VMEM((512, 512), F32)],
        compiler_params=pltpu.CompilerParams(vmem_limit_bytes=32 << 20),
    )(jnp.transpose(incoming), incoming.reshape(-1, LANE), pairs)
    return jnp.transpose(owned)


def exchange(x):
    return lax.all_to_all(x, ("gauss", "view"), split_axis=0, concat_axis=0, tiled=True)


def shards(table, view_proj, lengths, lists, requests, target):
    incoming = exchange(requests[0, 0])
    peers = incoming.shape[0]
    served = serve(incoming, table)
    pairs = exchange(served.reshape(peers, 32, LANE)).reshape(peers * 32, LANE)
    image, grads = render(lengths[0], lists[0], view_proj[0], pairs, target[0])
    returned = exchange(grads.reshape(peers, 32, LANE)).reshape(peers * 32, LANE)
    return image[None], collect(incoming, returned, table.shape[0])


def solution(mesh):
    return jax.shard_map(
        shards,
        mesh=mesh,
        in_specs=(
            P(("gauss", "view"), None),
            P("view", None, None),
            P("view", "gauss"),
            P("view", "gauss", None),
            P("view", "gauss", None, None),
            P("view", "gauss", None, None),
        ),
        out_specs=(P("view", "gauss", None, None), P(("gauss", "view"), None)),
        check_vma=False,
    )
```

```python
import functools

import functools

import jax
import jax.numpy as jnp
from jax import lax
from jax.experimental import pallas as pl
from jax.experimental.pallas import tpu as pltpu
from jax.sharding import PartitionSpec as P

LOG2E = 1.4426950408889634
FEATS = 57
ROW = 64
LANE = 128
PIX = 256
ACCS = 4
STEP = 256
RING = 9
PAD = 16
DRIP = 6
F32 = jnp.float32
BF16 = jnp.bfloat16


def split(x):
    hi = x.astype(BF16)
    lo = (x - hi.astype(F32)).astype(BF16)
    return hi, lo


def dot(a, b):
    return jnp.dot(a, b, preferred_element_type=F32)


def dot_t(a, b):
    return lax.dot_general(a, b, (((1,), (1,)), ((), ())), preferred_element_type=F32)


def unpack_rows(pairs_ref, rows_ref, peers):
    def step(i, c):
        for k in range(8):
            o = i * 8 + k
            two = pairs_ref[pl.ds(pl.multiple_of(o * 32, 32), 32), :].astype(F32)
            base = pl.multiple_of(o * 64, 64)
            rows_ref[pl.ds(base, 32), :] = two
            rows_ref[pl.ds(pl.multiple_of(base + 32, 32), 32), :] = pltpu.roll(two, 64, 1)
        return c

    lax.fori_loop(0, peers // 8, step, 0)


def pack_rows(accs, pairs_ref, peers):
    lane = lax.broadcasted_iota(jnp.int32, (32, LANE), 1)

    def step(i, c):
        for k in range(4):
            o = i * 4 + k
            base = pl.multiple_of(o * 64, 64)
            first = sum(acc[pl.ds(base, 32), :] for acc in accs)
            second = sum(acc[pl.ds(pl.multiple_of(base + 32, 32), 32), :] for acc in accs)
            pairs_ref[pl.ds(pl.multiple_of(o * 32, 32), 32), :] = jnp.where(
                lane < 64, first, pltpu.roll(second, 64, 1)
            )
        return c

    lax.fori_loop(0, peers // 4, step, 0)


def tiles_kernel(
    lens, lists, cam,
    pairs, target, prefix_mat, suffix_mat,
    image, out_pairs,
    base_of, tile_of, first_of, mirror_of, live_of,
    rows, acc0, acc1, acc2, acc3,
    splats, grows, feat_t, geo, weights, ratio, entering_ref, later_ref, pic, tgt, pull_rows, pull_t, grow_t,
    feat_new, geo_new, weights_new, ratio_new, rows_new, cols_new,
    dy_back, dy_front, qc_front, wide, wide_new,
):
    accs = (acc0, acc1, acc2, acc3)
    tiles = lens.shape[0]
    peers = pairs.shape[0] // 32
    entries = lists.shape[0] // (tiles + 1)

    def blank(i, c):
        base_of[i] = tiles * entries
        tile_of[i] = 0
        first_of[i] = 1
        mirror_of[i] = 0
        live_of[i] = 0
        return c

    lax.fori_loop(0, base_of.shape[0], blank, 0)

    def list_tile(t, at):
        steps = (lens[t] + STEP - 1) // STEP

        def list_step(j, c):
            where = at + j + PAD
            base_of[where] = t * entries + j * STEP
            tile_of[where] = t
            first_of[where] = jnp.where(j == 0, 1, 0)
            mirror_of[where] = at + steps - 1 - j
            live_of[where] = lens[t] - j * STEP
            return c

        lax.fori_loop(0, steps, list_step, 0)
        return at + steps

    count = lax.fori_loop(0, tiles, list_tile, 0)

    unpack_rows(pairs, rows, peers)
    rows[peers * 64:, :] = jnp.zeros((8, LANE), F32)

    def clear(i, c):
        for acc in accs:
            acc[pl.ds(pl.multiple_of(i * 64, 64), 64), :] = jnp.zeros((64, LANE), F32)
        return c

    lax.fori_loop(0, peers, clear, 0)
    tgt[...] = target[...].astype(F32)
    splats[...] = jnp.zeros_like(splats)
    feat_new[...] = jnp.zeros_like(feat_new)
    geo_new[...] = jnp.zeros_like(geo_new)

    prefix = prefix_mat[...]
    suffix = suffix_mat[...]
    sub16 = lax.broadcasted_iota(jnp.int32, (16, STEP), 0).astype(F32) + 0.5
    lane256 = lax.broadcasted_iota(jnp.int32, (1, STEP), 1)
    feature = lax.broadcasted_iota(jnp.int32, (64, PIX), 0) < FEATS

    def scatter(s):
        base = base_of[mirror_of[s + PAD] + PAD]
        base = jnp.where(live_of[s + PAD] > 0, base, tiles * entries)

        def rows_from(q):
            ids = [lists[base + q + k] for k in range(ACCS)]
            old = [accs[k][pl.ds(ids[k], 1), :] for k in range(ACCS)]
            for k in range(ACCS):
                accs[k][pl.ds(ids[k], 1), :] = old[k] + grows[q + k:q + k + 1, :]

        return [functools.partial(rows_from, q) for q in range(0, STEP, ACCS)]

    def turn_back():
        for k in range(2):
            part = jnp.concatenate(
                [grow_t[:, k * LANE:(k + 1) * LANE], jnp.zeros((64, LANE), F32)], axis=0
            )
            grows[k * LANE:(k + 1) * LANE, :] = jnp.transpose(part)

    def coords(g):
        return sub16 - geo[g, 0:1, :], sub16 - geo[g, 1:2, :]

    def spread(ref, cut):
        return jnp.stack([jnp.broadcast_to(ref[y:y + 1, cut], (16, LANE)) for y in range(16)])

    def backward(b, drip):
        f = mirror_of[b + PAD]
        g = f + 2
        slot = lax.rem(g, RING)
        t = tile_of[b + PAD]
        keep = first_of[b + PAD] == 0
        dx, dy = coords(g)
        dy_back[...] = dy
        ft = feat_t[g]
        halves = weights[slot]
        d_weight = dot(pull_t[t], jnp.concatenate([ft, ft], axis=0))
        quads = dot(pull_rows[t], halves)
        quads = quads[:64] + quads[64:]
        later = jnp.where(keep, later_ref[...], 0.0)
        sums = [None, None]
        for k in (1, 0):
            cut = slice(k * LANE, (k + 1) * LANE)
            prod = wide[slot, :, cut] * d_weight[:, cut]
            drip()
            both = dot(jnp.concatenate(split(prod), axis=1), suffix)
            drip()
            h = prod - ratio[slot, :, cut] * (both[:, :LANE] + later)
            drip()
            later = later + both[:, LANE:]
            drip()
            h = h.reshape(16, 16, LANE)
            dyk = spread(dy_back, cut)
            hy = h * dyk
            drip()
            sums[k] = (
                jnp.sum(h, axis=0),
                jnp.sum(hy, axis=0),
                jnp.sum(hy * dyk, axis=0),
            )
        later_ref[...] = later
        s0, s1, s2 = (jnp.concatenate([sums[0][j], sums[1][j]], axis=1) for j in range(3))
        sx = s0 * dx
        m0, mx, my, mxx, mxy, myy = (
            jnp.sum(m, axis=0, keepdims=True) for m in (s0, sx, s1, sx * dx, s1 * dx, s2)
        )
        ca, cb, cc = geo[g, 6:7, :], geo[g, 7:8, :], geo[g, 8:9, :]
        du = (ca * mx + cb * my) * geo[g, 9:10, :]
        dw = (cb * mx + cc * my) * geo[g, 10:11, :]
        shared = -0.5 * cb * mxy
        first = jnp.concatenate(
            [quads[:, 0:LANE] + quads[:, LANE:2 * LANE],
             quads[:, 2 * LANE:3 * LANE] + quads[:, 3 * LANE:]], axis=1
        )
        grow_t[0:56, :] = first[0:56]
        grow_t[56:57, :] = first[56:57]
        outs = (
            du * cam[0, 0] + dw * cam[1, 0],
            du * cam[0, 1] + dw * cam[1, 1],
            du * cam[0, 2] + dw * cam[1, 2],
            -0.5 * ca * mxx + shared,
            -0.5 * cc * myy + shared,
            -mxy * geo[g, 11:12, :],
            geo[g, 12:13, :] * m0,
        )
        for j, value in enumerate(outs):
            grow_t[57 + j:58 + j, :] = value

    def pull(p):
        t = tile_of[p + PAD]
        picture = pic[...]
        for h in range(2):
            image[h, pl.ds(t, FEATS, stride=tiles), :] = picture[:FEATS, h * LANE:(h + 1) * LANE]
        want = jnp.concatenate(
            [tgt[h, pl.ds(t, FEATS, stride=tiles), :] for h in range(2)], axis=1
        )
        want = jnp.concatenate([want, jnp.zeros((64 - FEATS, PIX), F32)], axis=0)
        diff = jnp.where(feature, picture - want, 0.0)
        hi, lo = split(diff)
        both = jnp.concatenate([hi, lo], axis=0)
        rows_new[...] = both
        cols_new[...] = jnp.transpose(both.astype(F32)).astype(BF16)

    def forward(f, drip):
        g = f + 2
        keep = first_of[f + PAD] == 0
        dx, dy = coords(g)
        qa = geo[g, 2:3, :] * dx * dx
        qb = geo[g, 3:4, :] * dx
        qc = geo[g, 4:5, :] * dy * dy + geo[g, 5:6, :]
        dy_front[...] = dy
        qc_front[...] = qc
        entering = jnp.where(keep, entering_ref[...], 0.0)
        parts = []
        for k in range(2):
            cut = slice(k * LANE, (k + 1) * LANE)
            power = qa[None, :, cut] + qb[None, :, cut] * spread(dy_front, cut) + spread(qc_front, cut)
            alpha = jnp.exp2(power.reshape(PIX, LANE))
            drip()
            rest = 1.0 - alpha
            logs = jnp.log2(rest)
            drip()
            both = dot(jnp.concatenate(split(logs), axis=1), prefix)
            drip()
            weight = alpha * jnp.exp2(both[:, :LANE] + entering)
            drip()
            entering = entering + both[:, LANE:]
            ratio_new[:, cut] = alpha * pl.reciprocal(rest, approx=True)
            wide_new[:, cut] = weight
            parts.extend(split(weight))
            drip()
        entering_ref[...] = entering
        halves = jnp.concatenate(parts, axis=1)
        weights_new[...] = halves
        ft = feat_t[g]
        left, right = ft[:, :LANE], ft[:, LANE:]
        pic[...] = jnp.where(keep, pic[...], 0.0) + dot_t(
            jnp.concatenate([left, left, right, right], axis=1), halves
        )

    def prepare(x):
        turned = [
            jnp.transpose(splats[k * LANE:(k + 1) * LANE, :])[0:64] for k in range(2)
        ]
        turned = jnp.concatenate(turned, axis=1)
        feat_new[...] = turned.astype(BF16)
        px, py, pz, sa, sc, sb, so = (turned[57 + j:58 + j, :] for j in range(7))
        tu = jnp.tanh(px * cam[0, 0] + py * cam[0, 1] + pz * cam[0, 2] + cam[0, 3])
        tw = jnp.tanh(px * cam[1, 0] + py * cam[1, 1] + pz * cam[1, 2] + cam[1, 3])
        ca, cc = jnp.exp(sa), jnp.exp(sc)
        tb = jnp.tanh(sb)
        root = 0.9 * jnp.sqrt(ca * cc)
        cb = tb * root
        soft = jnp.exp(-jnp.abs(so))
        log_o = jnp.minimum(so, 0.0) * LOG2E - jnp.log2(1.0 + soft)
        half = -0.5 * LOG2E
        values = (
            8.0 + 6.0 * tu,
            8.0 + 6.0 * tw,
            half * ca,
            (2.0 * half) * cb,
            half * cc,
            jnp.where(lane256 < live_of[x + PAD], log_o, -1e30),
            ca,
            cb,
            cc,
            6.0 * (1.0 - tu * tu),
            6.0 * (1.0 - tw * tw),
            root * (1.0 - tb * tb),
            jnp.where(so >= 0.0, soft, 1.0) / (1.0 + soft),
        )
        for j, value in enumerate(values):
            geo_new[j:j + 1, :] = value

    def gather(n):
        base = base_of[n + PAD]

        def rows_from(q):
            got = [rows[pl.ds(lists[base + q + j], 1), :] for j in range(4)]
            for j in range(4):
                splats[q + j:q + j + 1, :] = got[j]

        return [functools.partial(rows_from, q) for q in range(0, STEP, 4)]

    def file(n):
        feat_t[n] = feat_new[...]
        geo[n] = geo_new[...]
        slot = lax.rem(n + RING - 1, RING)
        weights[slot] = weights_new[...]
        ratio[slot] = ratio_new[...]
        wide[slot] = wide_new[...]
        t = tile_of[n - 4 + PAD]
        pull_rows[t] = rows_new[...]
        pull_t[t] = cols_new[...]

    moves = []

    def drip(share=1.0):
        for _ in range(min(len(moves), max(1, int(DRIP * share)))):
            moves.pop(0)()

    def flush():
        while moves:
            moves.pop(0)()

    def opening(n, c):
        file(n)
        pull(n - 3)
        prepare(n - 1)
        moves.extend(gather(n))
        forward(n - 2, drip)
        flush()
        return c

    def middle(n, c):
        file(n)
        turn_back()
        pull(n - 3)
        prepare(n - 1)
        for pair in zip(scatter(n - 8), gather(n)):
            moves.extend(pair)
        backward(n - 7, drip)
        forward(n - 2, drip)
        flush()
        return c

    def closing(n, c):
        turn_back()
        moves.extend(scatter(n - 8))
        backward(n - 7, drip)
        flush()
        return c

    lax.fori_loop(0, 7, opening, 0)
    lax.fori_loop(7, count + 3, middle, 0)
    file(count + 3)
    lax.fori_loop(count + 3, count + 8, closing, 0)
    pack_rows(accs, out_pairs, peers)


def triangles():
    r = lax.broadcasted_iota(jnp.int32, (PIX, PIX), 0) % LANE
    c = lax.broadcasted_iota(jnp.int32, (PIX, PIX), 1)
    prefix = (c >= LANE) | (r < c)
    suffix = (c >= LANE) | (r > c)
    return prefix.astype(BF16), suffix.astype(BF16)


def render(lens, lists, cam, pairs, target):
    tiles, entries = lists.shape
    peers = pairs.shape[0] // 32
    steps = tiles * (entries // STEP)
    live = lax.broadcasted_iota(jnp.int32, lists.shape, 1) < lens[:, None]
    flat = jnp.where(live, lists, peers * 64).reshape(-1)
    flat = jnp.concatenate([flat, jnp.full((entries,), peers * 64, jnp.int32)])
    smem = pl.BlockSpec(memory_space=pltpu.SMEM)
    vmem = pl.BlockSpec(memory_space=pltpu.VMEM)
    prefix, suffix = triangles()
    t2 = jnp.transpose(target, (1, 0, 2)).reshape(FEATS * tiles, PIX)
    t2 = jnp.stack([t2[:, :LANE], t2[:, LANE:]])
    image, grads = pl.pallas_call(
        tiles_kernel,
        out_shape=(
            jax.ShapeDtypeStruct((2, FEATS * tiles, LANE), F32),
            jax.ShapeDtypeStruct((peers * 32, LANE), F32),
        ),
        in_specs=[smem] * 3 + [vmem] * 4,
        out_specs=(vmem, vmem),
        scratch_shapes=[
            *[pltpu.SMEM((steps + 2 * PAD,), jnp.int32)] * 5,
            *[pltpu.VMEM((peers * 64 + 8, LANE), F32)] * (1 + ACCS),
            pltpu.VMEM((STEP, LANE), F32),
            pltpu.VMEM((STEP, LANE), F32),
            pltpu.VMEM((steps + 4, ROW, STEP), BF16),
            pltpu.VMEM((steps + 4, 16, STEP), F32),
            pltpu.VMEM((RING, PIX, 2 * STEP), BF16),
            pltpu.VMEM((RING, PIX, STEP), F32),
            pltpu.VMEM((PIX, LANE), F32),
            pltpu.VMEM((PIX, LANE), F32),
            pltpu.VMEM((64, PIX), F32),
            pltpu.VMEM((2, FEATS * tiles, LANE), F32),
            pltpu.VMEM((tiles, 2 * ROW, PIX), BF16),
            pltpu.VMEM((tiles, PIX, 2 * ROW), BF16),
            pltpu.VMEM((ROW, STEP), F32),
            pltpu.VMEM((ROW, STEP), BF16),
            pltpu.VMEM((16, STEP), F32),
            pltpu.VMEM((PIX, 2 * STEP), BF16),
            pltpu.VMEM((PIX, STEP), F32),
            pltpu.VMEM((2 * ROW, PIX), BF16),
            pltpu.VMEM((PIX, 2 * ROW), BF16),
            *[pltpu.VMEM((16, STEP), F32)] * 3,
            pltpu.VMEM((RING, PIX, STEP), F32),
            pltpu.VMEM((PIX, STEP), F32),
        ],
        compiler_params=pltpu.CompilerParams(vmem_limit_bytes=52 << 20),
    )(lens, flat, cam, pairs, t2, prefix, suffix)
    image = jnp.concatenate([image[0], image[1]], axis=1).reshape(FEATS, tiles, PIX)
    return jnp.transpose(image, (1, 0, 2)), grads


def serve_kernel(slot_major, table_lo, served):
    peers = slot_major.shape[1]
    lane = lax.broadcasted_iota(jnp.int32, (64, LANE), 1)
    upper = lane // 64
    mat = jnp.transpose(table_lo[...].astype(F32)).astype(BF16)

    def step(g, c):
        ids = pltpu.roll(slot_major[...], lax.rem(peers - g * 8, peers), 1)
        cols = [jnp.broadcast_to(ids[:, k:k + 1], (64, LANE)) for k in range(8)]
        hot = [
            jnp.concatenate(
                [jnp.where((col & 255) == lane + q * LANE, 1.0, 0.0).astype(BF16) for q in range(2)],
                axis=1,
            )
            for col in cols
        ]
        got = dot(jnp.concatenate(hot, axis=0), mat)
        for k in range(8):
            high = (cols[k] >> 8) - upper
            total = jnp.zeros((64, LANE), F32)
            for q in range(4):
                part = got[k * 64:(k + 1) * 64, q * LANE:(q + 1) * LANE]
                total = total + jnp.where(high == 2 * q, part, 0.0)
            total = total + pltpu.roll(total, 64, 1)
            out = jnp.where(lane[:32] < 64, total[:32], total[32:])
            served[pl.ds(pl.multiple_of((g * 8 + k) * 32, 32), 32), :] = out.astype(BF16)
        return c

    lax.fori_loop(0, peers // 8, step, 0)


def serve(incoming, table):
    peers = incoming.shape[0]
    turned = jnp.transpose(table)
    turned = jnp.concatenate([turned[ROW - FEATS:], turned[:ROW - FEATS]], axis=0)
    turned = turned.reshape(ROW, 8, PIX).transpose(1, 0, 2).reshape(8 * ROW, PIX)
    vmem = pl.BlockSpec(memory_space=pltpu.VMEM)
    return pl.pallas_call(
        serve_kernel,
        out_shape=jax.ShapeDtypeStruct((peers * 32, LANE), BF16),
        in_specs=[vmem, vmem],
        out_specs=vmem,
        compiler_params=pltpu.CompilerParams(vmem_limit_bytes=32 << 20),
    )(jnp.transpose(incoming), turned)


def collect_kernel(slot_major, flat, pairs, owned, total):
    peers = slot_major.shape[1]
    lane = lax.broadcasted_iota(jnp.int32, (64, LANE), 1)
    upper = lane // 64
    left = lane[:32] < 64
    low_id = lax.broadcasted_iota(jnp.int32, (512, LANE), 0)
    total[...] = jnp.zeros_like(total)

    def step(g, c):
        ids = pltpu.roll(slot_major[...], lax.rem(peers - g * 8, peers), 1)
        hot = []
        for k in range(4):
            row = flat[pl.ds(g * 4 + k, 1), :] & 511
            hot.append(jnp.where(low_id == row, 1.0, 0.0).astype(BF16))
        blocks = []
        for k in range(8):
            high = (jnp.broadcast_to(ids[:, k:k + 1], (64, LANE)) >> 9) - upper
            two = pairs[pl.ds(pl.multiple_of((g * 8 + k) * 32, 32), 32), :]
            other = pltpu.roll(two, 64, 1)
            both = jnp.concatenate(
                [jnp.where(left, two, other), jnp.where(left, other, two)], axis=0
            )
            hi = both.astype(BF16).astype(F32)
            parts = [
                jnp.where(high == 2 * q, part, 0.0).astype(BF16)
                for part in (hi, both - hi)
                for q in range(2)
            ]
            blocks.append(jnp.concatenate(parts, axis=1))
        total[...] += dot(jnp.concatenate(hot, axis=1), jnp.concatenate(blocks, axis=0))
        return c

    lax.fori_loop(0, peers // 8, step, 0)
    whole = jnp.transpose(total[:, :256] + total[:, 256:])
    for q in range(4):
        part = whole[q * 64:(q + 1) * 64]
        owned[:, q * 512:(q + 1) * 512] = jnp.concatenate([part[FEATS:], part[:FEATS]], axis=0)


def collect(incoming, pairs, rows):
    peers = incoming.shape[0]
    vmem = pl.BlockSpec(memory_space=pltpu.VMEM)
    owned = pl.pallas_call(
        collect_kernel,
        out_shape=jax.ShapeDtypeStruct((ROW, rows), F32),
        in_specs=[vmem] * 3,
        out_specs=vmem,
        scratch_shapes=[pltpu.VMEM((512, 512), F32)],
        compiler_params=pltpu.CompilerParams(vmem_limit_bytes=32 << 20),
    )(jnp.transpose(incoming), incoming.reshape(-1, LANE), pairs)
    return jnp.transpose(owned)


def exchange(x):
    return lax.all_to_all(x, ("gauss", "view"), split_axis=0, concat_axis=0, tiled=True)


def shards(table, view_proj, lengths, lists, requests, target):
    incoming = exchange(requests[0, 0])
    peers = incoming.shape[0]
    served = serve(incoming, table)
    pairs = exchange(served.reshape(peers, 32, LANE)).reshape(peers * 32, LANE)
    image, grads = render(lengths[0], lists[0], view_proj[0], pairs, target[0])
    returned = exchange(grads.reshape(peers, 32, LANE)).reshape(peers * 32, LANE)
    return image[None], collect(incoming, returned, table.shape[0])


def solution(mesh):
    return jax.shard_map(
        shards,
        mesh=mesh,
        in_specs=(
            P(("gauss", "view"), None),
            P("view", None, None),
            P("view", "gauss"),
            P("view", "gauss", None),
            P("view", "gauss", None, None),
            P("view", "gauss", None, None),
        ),
        out_specs=(P("view", "gauss", None, None), P(("gauss", "view"), None)),
        check_vma=False,
    )
```

```python
import functools

import functools

import jax
import jax.numpy as jnp
from jax import lax
from jax.experimental import pallas as pl
from jax.experimental.pallas import tpu as pltpu
from jax.sharding import PartitionSpec as P

LOG2E = 1.4426950408889634
FEATS = 57
ROW = 64
LANE = 128
PIX = 256
ACCS = 4
STEP = 256
RING = 9
PAD = 16
DRIP = 6
F32 = jnp.float32
BF16 = jnp.bfloat16


def split(x):
    hi = x.astype(BF16)
    lo = (x - hi.astype(F32)).astype(BF16)
    return hi, lo


def dot(a, b):
    return jnp.dot(a, b, preferred_element_type=F32)


def dot_t(a, b):
    return lax.dot_general(a, b, (((1,), (1,)), ((), ())), preferred_element_type=F32)


def unpack_rows(pairs_ref, rows_ref, peers):
    def step(i, c):
        for k in range(8):
            o = i * 8 + k
            two = pairs_ref[pl.ds(pl.multiple_of(o * 32, 32), 32), :].astype(F32)
            base = pl.multiple_of(o * 64, 64)
            rows_ref[pl.ds(base, 32), :] = two
            rows_ref[pl.ds(pl.multiple_of(base + 32, 32), 32), :] = pltpu.roll(two, 64, 1)
        return c

    lax.fori_loop(0, peers // 8, step, 0)


def pack_rows(accs, pairs_ref, peers):
    lane = lax.broadcasted_iota(jnp.int32, (32, LANE), 1)

    def step(i, c):
        for k in range(4):
            o = i * 4 + k
            base = pl.multiple_of(o * 64, 64)
            first = sum(acc[pl.ds(base, 32), :] for acc in accs)
            second = sum(acc[pl.ds(pl.multiple_of(base + 32, 32), 32), :] for acc in accs)
            pairs_ref[pl.ds(pl.multiple_of(o * 32, 32), 32), :] = jnp.where(
                lane < 64, first, pltpu.roll(second, 64, 1)
            )
        return c

    lax.fori_loop(0, peers // 4, step, 0)


def tiles_kernel(
    lens, lists, cam,
    pairs, target, prefix_mat, suffix_mat,
    image, out_pairs,
    base_of, tile_of, first_of, mirror_of, live_of,
    rows, acc0, acc1, acc2, acc3,
    splats, grows, feat_t, geo, weights, ratio, entering_ref, later_ref, pic, tgt, pull_rows, pull_t, grow_t,
    feat_new, geo_new, weights_new, ratio_new, rows_new, cols_new,
    dy_back, dy_front, qc_front, splats_new,
):
    accs = (acc0, acc1, acc2, acc3)
    tiles = lens.shape[0]
    peers = pairs.shape[0] // 32
    entries = lists.shape[0] // (tiles + 1)

    def blank(i, c):
        base_of[i] = tiles * entries
        tile_of[i] = 0
        first_of[i] = 1
        mirror_of[i] = 0
        live_of[i] = 0
        return c

    lax.fori_loop(0, base_of.shape[0], blank, 0)

    def list_tile(t, at):
        steps = (lens[t] + STEP - 1) // STEP

        def list_step(j, c):
            where = at + j + PAD
            base_of[where] = t * entries + j * STEP
            tile_of[where] = t
            first_of[where] = jnp.where(j == 0, 1, 0)
            mirror_of[where] = at + steps - 1 - j
            live_of[where] = lens[t] - j * STEP
            return c

        lax.fori_loop(0, steps, list_step, 0)
        return at + steps

    count = lax.fori_loop(0, tiles, list_tile, 0)

    unpack_rows(pairs, rows, peers)
    rows[peers * 64:, :] = jnp.zeros((8, LANE), F32)

    def clear(i, c):
        for acc in accs:
            acc[pl.ds(pl.multiple_of(i * 64, 64), 64), :] = jnp.zeros((64, LANE), F32)
        return c

    lax.fori_loop(0, peers, clear, 0)
    tgt[...] = target[...].astype(F32)
    splats_new[...] = jnp.zeros_like(splats_new)
    feat_new[...] = jnp.zeros_like(feat_new)
    geo_new[...] = jnp.zeros_like(geo_new)

    prefix = prefix_mat[...]
    suffix = suffix_mat[...]
    sub16 = lax.broadcasted_iota(jnp.int32, (16, STEP), 0).astype(F32) + 0.5
    lane256 = lax.broadcasted_iota(jnp.int32, (1, STEP), 1)
    feature = lax.broadcasted_iota(jnp.int32, (64, PIX), 0) < FEATS

    def scatter(s):
        base = base_of[mirror_of[s + PAD] + PAD]
        base = jnp.where(live_of[s + PAD] > 0, base, tiles * entries)

        def rows_from(q):
            ids = [lists[base + q + k] for k in range(ACCS)]
            old = [accs[k][pl.ds(ids[k], 1), :] for k in range(ACCS)]
            for k in range(ACCS):
                accs[k][pl.ds(ids[k], 1), :] = old[k] + grows[q + k:q + k + 1, :]

        return [functools.partial(rows_from, q) for q in range(0, STEP, ACCS)]

    def turn_back():
        for k in range(2):
            part = jnp.concatenate(
                [grow_t[:, k * LANE:(k + 1) * LANE], jnp.zeros((64, LANE), F32)], axis=0
            )
            grows[k * LANE:(k + 1) * LANE, :] = jnp.transpose(part)

    def coords(g):
        return sub16 - geo[g, 0:1, :], sub16 - geo[g, 1:2, :]

    def spread(ref, cut):
        return jnp.stack([jnp.broadcast_to(ref[y:y + 1, cut], (16, LANE)) for y in range(16)])

    def backward(b, drip):
        f = mirror_of[b + PAD]
        g = f + 2
        slot = lax.rem(g, RING)
        t = tile_of[b + PAD]
        keep = first_of[b + PAD] == 0
        dx, dy = coords(g)
        dy_back[...] = dy
        ft = feat_t[g]
        halves = weights[slot]
        d_weight = dot(pull_t[t], jnp.concatenate([ft, ft], axis=0))
        quads = dot(pull_rows[t], halves)
        quads = quads[:64] + quads[64:]
        later = jnp.where(keep, later_ref[...], 0.0)
        sums = [None, None]
        for k in (1, 0):
            cut = slice(k * LANE, (k + 1) * LANE)
            weight = (
                halves[:, 2 * k * LANE:(2 * k + 1) * LANE].astype(F32)
                + halves[:, (2 * k + 1) * LANE:(2 * k + 2) * LANE].astype(F32)
            )
            prod = weight * d_weight[:, cut]
            drip()
            both = dot(jnp.concatenate(split(prod), axis=1), suffix)
            drip()
            h = prod - ratio[slot, :, cut] * (both[:, :LANE] + later)
            drip()
            later = later + both[:, LANE:]
            drip()
            h = h.reshape(16, 16, LANE)
            dyk = spread(dy_back, cut)
            hy = h * dyk
            drip()
            sums[k] = (
                jnp.sum(h, axis=0),
                jnp.sum(hy, axis=0),
                jnp.sum(hy * dyk, axis=0),
            )
        later_ref[...] = later
        s0, s1, s2 = (jnp.concatenate([sums[0][j], sums[1][j]], axis=1) for j in range(3))
        sx = s0 * dx
        m0, mx, my, mxx, mxy, myy = (
            jnp.sum(m, axis=0, keepdims=True) for m in (s0, sx, s1, sx * dx, s1 * dx, s2)
        )
        ca, cb, cc = geo[g, 6:7, :], geo[g, 7:8, :], geo[g, 8:9, :]
        du = (ca * mx + cb * my) * geo[g, 9:10, :]
        dw = (cb * mx + cc * my) * geo[g, 10:11, :]
        shared = -0.5 * cb * mxy
        first = jnp.concatenate(
            [quads[:, 0:LANE] + quads[:, LANE:2 * LANE],
             quads[:, 2 * LANE:3 * LANE] + quads[:, 3 * LANE:]], axis=1
        )
        grow_t[0:56, :] = first[0:56]
        grow_t[56:57, :] = first[56:57]
        outs = (
            du * cam[0, 0] + dw * cam[1, 0],
            du * cam[0, 1] + dw * cam[1, 1],
            du * cam[0, 2] + dw * cam[1, 2],
            -0.5 * ca * mxx + shared,
            -0.5 * cc * myy + shared,
            -mxy * geo[g, 11:12, :],
            geo[g, 12:13, :] * m0,
        )
        for j, value in enumerate(outs):
            grow_t[57 + j:58 + j, :] = value

    def pull(p):
        t = tile_of[p + PAD]
        picture = pic[...]
        for h in range(2):
            image[h, pl.ds(t, FEATS, stride=tiles), :] = picture[:FEATS, h * LANE:(h + 1) * LANE]
        want = jnp.concatenate(
            [tgt[h, pl.ds(t, FEATS, stride=tiles), :] for h in range(2)], axis=1
        )
        want = jnp.concatenate([want, jnp.zeros((64 - FEATS, PIX), F32)], axis=0)
        diff = jnp.where(feature, picture - want, 0.0)
        hi, lo = split(diff)
        both = jnp.concatenate([hi, lo], axis=0)
        rows_new[...] = both
        cols_new[...] = jnp.transpose(both.astype(F32)).astype(BF16)

    def forward(f, drip):
        g = f + 2
        keep = first_of[f + PAD] == 0
        dx, dy = coords(g)
        qa = geo[g, 2:3, :] * dx * dx
        qb = geo[g, 3:4, :] * dx
        qc = geo[g, 4:5, :] * dy * dy + geo[g, 5:6, :]
        dy_front[...] = dy
        qc_front[...] = qc
        entering = jnp.where(keep, entering_ref[...], 0.0)
        parts = []
        for k in range(2):
            cut = slice(k * LANE, (k + 1) * LANE)
            power = qa[None, :, cut] + qb[None, :, cut] * spread(dy_front, cut) + spread(qc_front, cut)
            alpha = jnp.exp2(power.reshape(PIX, LANE))
            drip()
            rest = 1.0 - alpha
            logs = jnp.log2(rest)
            drip()
            both = dot(jnp.concatenate(split(logs), axis=1), prefix)
            drip()
            weight = alpha * jnp.exp2(both[:, :LANE] + entering)
            drip()
            entering = entering + both[:, LANE:]
            ratio_new[:, cut] = alpha * pl.reciprocal(rest, approx=True)
            parts.extend(split(weight))
            drip()
        entering_ref[...] = entering
        halves = jnp.concatenate(parts, axis=1)
        weights_new[...] = halves
        ft = feat_t[g]
        left, right = ft[:, :LANE], ft[:, LANE:]
        pic[...] = jnp.where(keep, pic[...], 0.0) + dot_t(
            jnp.concatenate([left, left, right, right], axis=1), halves
        )

    def prepare(x):
        turned = [
            jnp.transpose(splats[k * LANE:(k + 1) * LANE, :])[0:64] for k in range(2)
        ]
        turned = jnp.concatenate(turned, axis=1)
        feat_new[...] = turned.astype(BF16)
        px, py, pz, sa, sc, sb, so = (turned[57 + j:58 + j, :] for j in range(7))
        tu = jnp.tanh(px * cam[0, 0] + py * cam[0, 1] + pz * cam[0, 2] + cam[0, 3])
        tw = jnp.tanh(px * cam[1, 0] + py * cam[1, 1] + pz * cam[1, 2] + cam[1, 3])
        ca, cc = jnp.exp(sa), jnp.exp(sc)
        tb = jnp.tanh(sb)
        root = 0.9 * jnp.sqrt(ca * cc)
        cb = tb * root
        soft = jnp.exp(-jnp.abs(so))
        log_o = jnp.minimum(so, 0.0) * LOG2E - jnp.log2(1.0 + soft)
        half = -0.5 * LOG2E
        values = (
            8.0 + 6.0 * tu,
            8.0 + 6.0 * tw,
            half * ca,
            (2.0 * half) * cb,
            half * cc,
            jnp.where(lane256 < live_of[x + PAD], log_o, -1e30),
            ca,
            cb,
            cc,
            6.0 * (1.0 - tu * tu),
            6.0 * (1.0 - tw * tw),
            root * (1.0 - tb * tb),
            jnp.where(so >= 0.0, soft, 1.0) / (1.0 + soft),
        )
        for j, value in enumerate(values):
            geo_new[j:j + 1, :] = value

    def gather(n):
        base = base_of[n + PAD]

        def rows_from(q):
            got = [rows[pl.ds(lists[base + q + j], 1), :] for j in range(4)]
            for j in range(4):
                splats_new[q + j:q + j + 1, :] = got[j]

        return [functools.partial(rows_from, q) for q in range(0, STEP, 4)]

    def file(n):
        feat_t[n] = feat_new[...]
        geo[n] = geo_new[...]
        slot = lax.rem(n + RING - 1, RING)
        weights[slot] = weights_new[...]
        ratio[slot] = ratio_new[...]
        t = tile_of[n - 4 + PAD]
        pull_rows[t] = rows_new[...]
        pull_t[t] = cols_new[...]

    moves = []

    def drip(share=1.0):
        for _ in range(min(len(moves), max(1, int(DRIP * share)))):
            moves.pop(0)()

    def flush():
        while moves:
            moves.pop(0)()

    def opening(n, c):
        splats[...] = splats_new[...]
        file(n)
        pull(n - 3)
        prepare(n - 1)
        moves.extend(gather(n))
        forward(n - 2, drip)
        flush()
        return c

    def middle(n, c):
        @pl.when(n > 0)
        def _():
            splats[...] = splats_new[...]

        file(n)
        turn_back()

        prepare(n - 1)
        pull(n - 3)
        for pair in zip(scatter(n - 8), gather(n)):
            moves.extend(pair)
        forward(n - 2, drip)
        backward(n - 7, drip)
        flush()
        return c

    def closing(n, c):
        turn_back()
        moves.extend(scatter(n - 8))
        backward(n - 7, drip)
        flush()
        return c

    lax.fori_loop(0, 7, opening, 0)
    lax.fori_loop(7, count + 3, middle, 0)
    file(count + 3)
    lax.fori_loop(count + 3, count + 8, closing, 0)
    pack_rows(accs, out_pairs, peers)


def triangles():
    r = lax.broadcasted_iota(jnp.int32, (PIX, PIX), 0) % LANE
    c = lax.broadcasted_iota(jnp.int32, (PIX, PIX), 1)
    prefix = (c >= LANE) | (r < c)
    suffix = (c >= LANE) | (r > c)
    return prefix.astype(BF16), suffix.astype(BF16)


def render(lens, lists, cam, pairs, target):
    tiles, entries = lists.shape
    peers = pairs.shape[0] // 32
    steps = tiles * (entries // STEP)
    live = lax.broadcasted_iota(jnp.int32, lists.shape, 1) < lens[:, None]
    flat = jnp.where(live, lists, peers * 64).reshape(-1)
    flat = jnp.concatenate([flat, jnp.full((entries,), peers * 64, jnp.int32)])
    smem = pl.BlockSpec(memory_space=pltpu.SMEM)
    vmem = pl.BlockSpec(memory_space=pltpu.VMEM)
    prefix, suffix = triangles()
    t2 = jnp.transpose(target, (1, 0, 2)).reshape(FEATS * tiles, PIX)
    t2 = jnp.stack([t2[:, :LANE], t2[:, LANE:]])
    image, grads = pl.pallas_call(
        tiles_kernel,
        out_shape=(
            jax.ShapeDtypeStruct((2, FEATS * tiles, LANE), F32),
            jax.ShapeDtypeStruct((peers * 32, LANE), F32),
        ),
        in_specs=[smem] * 3 + [vmem] * 4,
        out_specs=(vmem, vmem),
        scratch_shapes=[
            *[pltpu.SMEM((steps + 2 * PAD,), jnp.int32)] * 5,
            *[pltpu.VMEM((peers * 64 + 8, LANE), F32)] * (1 + ACCS),
            pltpu.VMEM((STEP, LANE), F32),
            pltpu.VMEM((STEP, LANE), F32),
            pltpu.VMEM((steps + 4, ROW, STEP), BF16),
            pltpu.VMEM((steps + 4, 16, STEP), F32),
            pltpu.VMEM((RING, PIX, 2 * STEP), BF16),
            pltpu.VMEM((RING, PIX, STEP), F32),
            pltpu.VMEM((PIX, LANE), F32),
            pltpu.VMEM((PIX, LANE), F32),
            pltpu.VMEM((64, PIX), F32),
            pltpu.VMEM((2, FEATS * tiles, LANE), F32),
            pltpu.VMEM((tiles, 2 * ROW, PIX), BF16),
            pltpu.VMEM((tiles, PIX, 2 * ROW), BF16),
            pltpu.VMEM((ROW, STEP), F32),
            pltpu.VMEM((ROW, STEP), BF16),
            pltpu.VMEM((16, STEP), F32),
            pltpu.VMEM((PIX, 2 * STEP), BF16),
            pltpu.VMEM((PIX, STEP), F32),
            pltpu.VMEM((2 * ROW, PIX), BF16),
            pltpu.VMEM((PIX, 2 * ROW), BF16),
            *[pltpu.VMEM((16, STEP), F32)] * 3,
            pltpu.VMEM((STEP, LANE), F32),
        ],
        compiler_params=pltpu.CompilerParams(vmem_limit_bytes=52 << 20),
    )(lens, flat, cam, pairs, t2, prefix, suffix)
    image = jnp.concatenate([image[0], image[1]], axis=1).reshape(FEATS, tiles, PIX)
    return jnp.transpose(image, (1, 0, 2)), grads


def serve_kernel(slot_major, table_lo, served):
    peers = slot_major.shape[1]
    lane = lax.broadcasted_iota(jnp.int32, (64, LANE), 1)
    upper = lane // 64
    mat = jnp.transpose(table_lo[...].astype(F32)).astype(BF16)

    def step(g, c):
        ids = pltpu.roll(slot_major[...], lax.rem(peers - g * 32, peers), 1)
        cols = [jnp.broadcast_to(ids[:, k:k + 1], (64, LANE)) for k in range(32)]
        hot = [
            jnp.concatenate(
                [jnp.where((col & 255) == lane + q * LANE, 1.0, 0.0).astype(BF16) for q in range(2)],
                axis=1,
            )
            for col in cols
        ]
        got = dot(jnp.concatenate(hot, axis=0), mat)
        for k in range(32):
            high = (cols[k] >> 8) - upper
            total = jnp.zeros((64, LANE), F32)
            for q in range(4):
                part = got[k * 64:(k + 1) * 64, q * LANE:(q + 1) * LANE]
                total = total + jnp.where(high == 2 * q, part, 0.0)
            total = total + pltpu.roll(total, 64, 1)
            out = jnp.where(lane[:32] < 64, total[:32], total[32:])
            served[pl.ds(pl.multiple_of((g * 32 + k) * 32, 32), 32), :] = out.astype(BF16)
        return c

    lax.fori_loop(0, peers // 32, step, 0)


def serve(incoming, table):
    peers = incoming.shape[0]
    turned = jnp.transpose(table)
    turned = jnp.concatenate([turned[ROW - FEATS:], turned[:ROW - FEATS]], axis=0)
    turned = turned.reshape(ROW, 8, PIX).transpose(1, 0, 2).reshape(8 * ROW, PIX)
    vmem = pl.BlockSpec(memory_space=pltpu.VMEM)
    return pl.pallas_call(
        serve_kernel,
        out_shape=jax.ShapeDtypeStruct((peers * 32, LANE), BF16),
        in_specs=[vmem, vmem],
        out_specs=vmem,
        compiler_params=pltpu.CompilerParams(vmem_limit_bytes=32 << 20),
    )(jnp.transpose(incoming), turned)


def collect_kernel(slot_major, flat, pairs, owned, total):
    peers = slot_major.shape[1]
    lane = lax.broadcasted_iota(jnp.int32, (64, LANE), 1)
    upper = lane // 64
    left = lane[:32] < 64
    low_id = lax.broadcasted_iota(jnp.int32, (512, LANE), 0)
    total[...] = jnp.zeros_like(total)

    def step(g, c):
        ids = pltpu.roll(slot_major[...], lax.rem(peers - g * 32, peers), 1)
        hot = []
        for k in range(16):
            row = flat[pl.ds(g * 16 + k, 1), :] & 511
            hot.append(jnp.where(low_id == row, 1.0, 0.0).astype(BF16))
        blocks = []
        for k in range(32):
            high = (jnp.broadcast_to(ids[:, k:k + 1], (64, LANE)) >> 9) - upper
            two = pairs[pl.ds(pl.multiple_of((g * 32 + k) * 32, 32), 32), :]
            other = pltpu.roll(two, 64, 1)
            both = jnp.concatenate(
                [jnp.where(left, two, other), jnp.where(left, other, two)], axis=0
            )
            hi = both.astype(BF16).astype(F32)
            parts = [
                jnp.where(high == 2 * q, part, 0.0).astype(BF16)
                for part in (hi, both - hi)
                for q in range(2)
            ]
            blocks.append(jnp.concatenate(parts, axis=1))
        total[...] += dot(jnp.concatenate(hot, axis=1), jnp.concatenate(blocks, axis=0))
        return c

    lax.fori_loop(0, peers // 32, step, 0)
    whole = jnp.transpose(total[:, :256] + total[:, 256:])
    for q in range(4):
        part = whole[q * 64:(q + 1) * 64]
        owned[:, q * 512:(q + 1) * 512] = jnp.concatenate([part[FEATS:], part[:FEATS]], axis=0)


def collect(incoming, pairs, rows):
    peers = incoming.shape[0]
    vmem = pl.BlockSpec(memory_space=pltpu.VMEM)
    owned = pl.pallas_call(
        collect_kernel,
        out_shape=jax.ShapeDtypeStruct((ROW, rows), F32),
        in_specs=[vmem] * 3,
        out_specs=vmem,
        scratch_shapes=[pltpu.VMEM((512, 512), F32)],
        compiler_params=pltpu.CompilerParams(vmem_limit_bytes=32 << 20),
    )(jnp.transpose(incoming), incoming.reshape(-1, LANE), pairs)
    return jnp.transpose(owned)


def exchange(x):
    return lax.all_to_all(x, ("gauss", "view"), split_axis=0, concat_axis=0, tiled=True)


def shards(table, view_proj, lengths, lists, requests, target):
    incoming = exchange(requests[0, 0])
    peers = incoming.shape[0]
    served = serve(incoming, table)
    pairs = exchange(served.reshape(peers, 32, LANE)).reshape(peers * 32, LANE)
    image, grads = render(lengths[0], lists[0], view_proj[0], pairs, target[0])
    returned = exchange(grads.reshape(peers, 32, LANE)).reshape(peers * 32, LANE)
    return image[None], collect(incoming, returned, table.shape[0])


def solution(mesh):
    return jax.shard_map(
        shards,
        mesh=mesh,
        in_specs=(
            P(("gauss", "view"), None),
            P("view", None, None),
            P("view", "gauss"),
            P("view", "gauss", None),
            P("view", "gauss", None, None),
            P("view", "gauss", None, None),
        ),
        out_specs=(P("view", "gauss", None, None), P(("gauss", "view"), None)),
        check_vma=False,
    )
```

```python
import functools

import functools

import jax
import jax.numpy as jnp
from jax import lax
from jax.experimental import pallas as pl
from jax.experimental.pallas import tpu as pltpu
from jax.sharding import PartitionSpec as P

LOG2E = 1.4426950408889634
FEATS = 57
ROW = 64
LANE = 128
PIX = 256
ACCS = 4
STEP = 256
RING = 9
PAD = 16
ORDER = "fbfbfbfbfb"
ONE = ""
DRIP = 6
F32 = jnp.float32
BF16 = jnp.bfloat16


def split(x):
    hi = x.astype(BF16)
    lo = (x - hi.astype(F32)).astype(BF16)
    return hi, lo


def dot(a, b):
    return jnp.dot(a, b, preferred_element_type=F32)


def dot_t(a, b):
    return lax.dot_general(a, b, (((1,), (1,)), ((), ())), preferred_element_type=F32)


def unpack_rows(pairs_ref, rows_ref, peers):
    def step(i, c):
        for k in range(8):
            o = i * 8 + k
            two = pairs_ref[pl.ds(pl.multiple_of(o * 32, 32), 32), :].astype(F32)
            base = pl.multiple_of(o * 64, 64)
            rows_ref[pl.ds(base, 32), :] = two
            rows_ref[pl.ds(pl.multiple_of(base + 32, 32), 32), :] = pltpu.roll(two, 64, 1)
        return c

    lax.fori_loop(0, peers // 8, step, 0)


def pack_rows(accs, pairs_ref, out_ref, sem, peers):
    lane = lax.broadcasted_iota(jnp.int32, (32, LANE), 1)

    def step(i, c):
        for k in range(8):
            o = i * 8 + k
            base = pl.multiple_of(o * 64, 64)
            first = sum(acc[pl.ds(base, 32), :] for acc in accs)
            second = sum(acc[pl.ds(pl.multiple_of(base + 32, 32), 32), :] for acc in accs)
            pairs_ref[pl.ds(pl.multiple_of(o * 32, 32), 32), :] = jnp.where(
                lane < 64, first, pltpu.roll(second, 64, 1)
            )
        part = pl.ds(pl.multiple_of(i * 256, 256), 256)
        pltpu.make_async_copy(pairs_ref.at[part], out_ref.at[part], sem).start()
        return c

    lax.fori_loop(0, peers // 8, step, 0)
    pltpu.make_async_copy(pairs_ref, out_ref, sem).wait()


def tiles_kernel(
    lens, lists, cam,
    pairs, target, prefix_mat, suffix_mat,
    image, out_pairs,
    base_of, tile_of, first_of, mirror_of, live_of,
    rows, acc0, acc1, acc2, acc3,
    splats, grows, feat_t, geo, weights, ratio, entering_ref, later_ref, pic, tgt, pull_rows, pull_t, grow_t,
    feat_new, geo_new, weights_new, ratio_new, rows_new, cols_new,
    dy_back, dy_front, qc_front, splats_new, packed, sem,
):
    accs = (acc0, acc1, acc2, acc3)
    tiles = lens.shape[0]
    peers = pairs.shape[0] // 32
    entries = lists.shape[0] // (tiles + 1)

    def blank(i, c):
        base_of[i] = tiles * entries
        tile_of[i] = 0
        first_of[i] = 1
        mirror_of[i] = 0
        live_of[i] = 0
        return c

    lax.fori_loop(0, base_of.shape[0], blank, 0)

    def list_tile(t, at):
        steps = (lens[t] + STEP - 1) // STEP

        def list_step(j, c):
            where = at + j + PAD
            base_of[where] = t * entries + j * STEP
            tile_of[where] = t
            first_of[where] = jnp.where(j == 0, 1, 0)
            mirror_of[where] = at + steps - 1 - j
            live_of[where] = lens[t] - j * STEP
            return c

        lax.fori_loop(0, steps, list_step, 0)
        return at + steps

    count = lax.fori_loop(0, tiles, list_tile, 0)

    unpack_rows(pairs, rows, peers)
    rows[peers * 64:, :] = jnp.zeros((8, LANE), F32)

    def clear(i, c):
        for acc in accs:
            acc[pl.ds(pl.multiple_of(i * 64, 64), 64), :] = jnp.zeros((64, LANE), F32)
        return c

    lax.fori_loop(0, peers, clear, 0)
    tgt[...] = target[...].astype(F32)
    splats_new[...] = jnp.zeros_like(splats_new)
    feat_new[...] = jnp.zeros_like(feat_new)
    geo_new[...] = jnp.zeros_like(geo_new)

    prefix = prefix_mat[...]
    suffix = suffix_mat[...]
    sub16 = lax.broadcasted_iota(jnp.int32, (16, STEP), 0).astype(F32) + 0.5
    lane256 = lax.broadcasted_iota(jnp.int32, (1, STEP), 1)
    feature = lax.broadcasted_iota(jnp.int32, (64, PIX), 0) < FEATS

    def scatter(s):
        base = base_of[mirror_of[s + PAD] + PAD]
        base = jnp.where(live_of[s + PAD] > 0, base, tiles * entries)

        def rows_from(q):
            ids = [lists[base + q + k] for k in range(ACCS)]
            old = [accs[k][pl.ds(ids[k], 1), :] for k in range(ACCS)]
            for k in range(ACCS):
                accs[k][pl.ds(ids[k], 1), :] = old[k] + grows[q + k:q + k + 1, :]

        return [functools.partial(rows_from, q) for q in range(0, STEP, ACCS)]

    def turn_back():
        for k in range(2):
            part = jnp.concatenate(
                [grow_t[:, k * LANE:(k + 1) * LANE], jnp.zeros((64, LANE), F32)], axis=0
            )
            grows[k * LANE:(k + 1) * LANE, :] = jnp.transpose(part)

    def coords(g):
        return sub16 - geo[g, 0:1, :], sub16 - geo[g, 1:2, :]

    def spread(ref, cut):
        return jnp.stack([jnp.broadcast_to(ref[y:y + 1, cut], (16, LANE)) for y in range(16)])

    def backward(b, drip):
        f = mirror_of[b + PAD]
        g = f + 2
        slot = lax.rem(g, RING)
        t = tile_of[b + PAD]
        keep = first_of[b + PAD] == 0
        dx, dy = coords(g)
        dy_back[...] = dy
        ft = feat_t[g]
        halves = weights[slot]
        d_weight = dot(pull_t[t], jnp.concatenate([ft, ft], axis=0))
        quads = dot(pull_rows[t], halves)
        quads = quads[:64] + quads[64:]
        yield
        prods, boths, sums = [None, None], [None, None], [None, None]
        for k in (1, 0):
            cut = slice(k * LANE, (k + 1) * LANE)
            weight = (
                halves[:, 2 * k * LANE:(2 * k + 1) * LANE].astype(F32)
                + halves[:, (2 * k + 1) * LANE:(2 * k + 2) * LANE].astype(F32)
            )
            prods[k] = weight * d_weight[:, cut]
            drip()
            boths[k] = dot(jnp.concatenate(split(prods[k]), axis=1), suffix)
            drip()
            yield
        later = jnp.where(keep, later_ref[...], 0.0)
        for k in (1, 0):
            cut = slice(k * LANE, (k + 1) * LANE)
            h = prods[k] - ratio[slot, :, cut] * (boths[k][:, :LANE] + later)
            drip()
            later = later + boths[k][:, LANE:]
            drip()
            h = h.reshape(16, 16, LANE)
            dyk = spread(dy_back, cut)
            hy = h * dyk
            drip()
            sums[k] = (
                jnp.sum(h, axis=0),
                jnp.sum(hy, axis=0),
                jnp.sum(hy * dyk, axis=0),
            )
            yield
        later_ref[...] = later
        s0, s1, s2 = (jnp.concatenate([sums[0][j], sums[1][j]], axis=1) for j in range(3))
        sx = s0 * dx
        m0, mx, my, mxx, mxy, myy = (
            jnp.sum(m, axis=0, keepdims=True) for m in (s0, sx, s1, sx * dx, s1 * dx, s2)
        )
        ca, cb, cc = geo[g, 6:7, :], geo[g, 7:8, :], geo[g, 8:9, :]
        du = (ca * mx + cb * my) * geo[g, 9:10, :]
        dw = (cb * mx + cc * my) * geo[g, 10:11, :]
        shared = -0.5 * cb * mxy
        first = jnp.concatenate(
            [quads[:, 0:LANE] + quads[:, LANE:2 * LANE],
             quads[:, 2 * LANE:3 * LANE] + quads[:, 3 * LANE:]], axis=1
        )
        grow_t[0:56, :] = first[0:56]
        grow_t[56:57, :] = first[56:57]
        outs = (
            du * cam[0, 0] + dw * cam[1, 0],
            du * cam[0, 1] + dw * cam[1, 1],
            du * cam[0, 2] + dw * cam[1, 2],
            -0.5 * ca * mxx + shared,
            -0.5 * cc * myy + shared,
            -mxy * geo[g, 11:12, :],
            geo[g, 12:13, :] * m0,
        )
        for j, value in enumerate(outs):
            grow_t[57 + j:58 + j, :] = value

    def pull(p):
        t = tile_of[p + PAD]
        picture = pic[...]
        for h in range(2):
            image[h, pl.ds(t, FEATS, stride=tiles), :] = picture[:FEATS, h * LANE:(h + 1) * LANE]
        want = jnp.concatenate(
            [tgt[h, pl.ds(t, FEATS, stride=tiles), :] for h in range(2)], axis=1
        )
        want = jnp.concatenate([want, jnp.zeros((64 - FEATS, PIX), F32)], axis=0)
        diff = jnp.where(feature, picture - want, 0.0)
        hi, lo = split(diff)
        both = jnp.concatenate([hi, lo], axis=0)
        rows_new[...] = both
        cols_new[...] = jnp.transpose(both.astype(F32)).astype(BF16)

    def forward(f, drip):
        g = f + 2
        keep = first_of[f + PAD] == 0
        dx, dy = coords(g)
        qa = geo[g, 2:3, :] * dx * dx
        qb = geo[g, 3:4, :] * dx
        qc = geo[g, 4:5, :] * dy * dy + geo[g, 5:6, :]
        dy_front[...] = dy
        qc_front[...] = qc
        entering = jnp.where(keep, entering_ref[...], 0.0)
        parts, kept = [], []
        for k in range(2):
            cut = slice(k * LANE, (k + 1) * LANE)
            power = qa[None, :, cut] + qb[None, :, cut] * spread(dy_front, cut) + spread(qc_front, cut)
            alpha = jnp.exp2(power.reshape(PIX, LANE))
            drip()
            rest = 1.0 - alpha
            logs = jnp.log2(rest)
            drip()
            both = dot(jnp.concatenate(split(logs), axis=1), prefix)
            ratio_new[:, cut] = alpha * pl.reciprocal(rest, approx=True)
            drip()
            kept.append((alpha, both))
            yield
        for alpha, both in kept:
            weight = alpha * jnp.exp2(both[:, :LANE] + entering)
            drip()
            entering = entering + both[:, LANE:]
            parts.extend(split(weight))
            drip()
            yield
        entering_ref[...] = entering
        halves = jnp.concatenate(parts, axis=1)
        weights_new[...] = halves
        ft = feat_t[g]
        left, right = ft[:, :LANE], ft[:, LANE:]
        pic[...] = jnp.where(keep, pic[...], 0.0) + dot_t(
            jnp.concatenate([left, left, right, right], axis=1), halves
        )

    def prepare(x):
        turned = [
            jnp.transpose(splats[k * LANE:(k + 1) * LANE, :])[0:64] for k in range(2)
        ]
        turned = jnp.concatenate(turned, axis=1)
        feat_new[...] = turned.astype(BF16)
        px, py, pz, sa, sc, sb, so = (turned[57 + j:58 + j, :] for j in range(7))
        tu = jnp.tanh(px * cam[0, 0] + py * cam[0, 1] + pz * cam[0, 2] + cam[0, 3])
        tw = jnp.tanh(px * cam[1, 0] + py * cam[1, 1] + pz * cam[1, 2] + cam[1, 3])
        ca, cc = jnp.exp(sa), jnp.exp(sc)
        tb = jnp.tanh(sb)
        root = 0.9 * jnp.sqrt(ca * cc)
        cb = tb * root
        soft = jnp.exp(-jnp.abs(so))
        log_o = jnp.minimum(so, 0.0) * LOG2E - jnp.log2(1.0 + soft)
        half = -0.5 * LOG2E
        values = (
            8.0 + 6.0 * tu,
            8.0 + 6.0 * tw,
            half * ca,
            (2.0 * half) * cb,
            half * cc,
            jnp.where(lane256 < live_of[x + PAD], log_o, -1e30),
            ca,
            cb,
            cc,
            6.0 * (1.0 - tu * tu),
            6.0 * (1.0 - tw * tw),
            root * (1.0 - tb * tb),
            jnp.where(so >= 0.0, soft, 1.0) / (1.0 + soft),
        )
        for j, value in enumerate(values):
            geo_new[j:j + 1, :] = value

    def gather(n):
        base = base_of[n + PAD]

        def rows_from(q):
            got = [rows[pl.ds(lists[base + q + j], 1), :] for j in range(4)]
            for j in range(4):
                splats_new[q + j:q + j + 1, :] = got[j]

        return [functools.partial(rows_from, q) for q in range(0, STEP, 4)]

    def file(n):
        feat_t[n] = feat_new[...]
        geo[n] = geo_new[...]
        slot = lax.rem(n + RING - 1, RING)
        weights[slot] = weights_new[...]
        ratio[slot] = ratio_new[...]
        t = tile_of[n - 4 + PAD]
        pull_rows[t] = rows_new[...]
        pull_t[t] = cols_new[...]

    moves = []

    def drip(share=1.0):
        for _ in range(min(len(moves), max(1, int(DRIP * share)))):
            moves.pop(0)()

    def flush():
        while moves:
            moves.pop(0)()

    def run(order, front, back):
        for letter in order:
            stage = front if letter == "f" else back
            if stage is not None:
                next(stage, None)
        for stage in (front, back):
            if stage is not None:
                for _ in stage:
                    pass

    def opening(n, c):
        splats[...] = splats_new[...]
        file(n)
        pull(n - 3)
        prepare(n - 1)
        moves.extend(gather(n))
        run(ONE, forward(n - 2, drip), None)
        flush()
        return c

    def middle(n, c):
        @pl.when(n > 0)
        def _():
            splats[...] = splats_new[...]

        file(n)
        turn_back()

        prepare(n - 1)
        pull(n - 3)
        for pair in zip(scatter(n - 8), gather(n)):
            moves.extend(pair)
        run(ORDER, forward(n - 2, drip), backward(n - 7, drip))
        flush()
        return c

    def closing(n, c):
        turn_back()
        moves.extend(scatter(n - 8))
        run(ONE, None, backward(n - 7, drip))
        flush()
        return c

    lax.fori_loop(0, 7, opening, 0)
    lax.fori_loop(7, count + 3, middle, 0)
    file(count + 3)
    lax.fori_loop(count + 3, count + 8, closing, 0)
    pack_rows(accs, packed, out_pairs, sem, peers)


def triangles():
    r = lax.broadcasted_iota(jnp.int32, (PIX, PIX), 0) % LANE
    c = lax.broadcasted_iota(jnp.int32, (PIX, PIX), 1)
    prefix = (c >= LANE) | (r < c)
    suffix = (c >= LANE) | (r > c)
    return prefix.astype(BF16), suffix.astype(BF16)


def render(lens, lists, cam, pairs, target):
    tiles, entries = lists.shape
    peers = pairs.shape[0] // 32
    steps = tiles * (entries // STEP)
    live = lax.broadcasted_iota(jnp.int32, lists.shape, 1) < lens[:, None]
    flat = jnp.where(live, lists, peers * 64).reshape(-1)
    flat = jnp.concatenate([flat, jnp.full((entries,), peers * 64, jnp.int32)])
    smem = pl.BlockSpec(memory_space=pltpu.SMEM)
    vmem = pl.BlockSpec(memory_space=pltpu.VMEM)
    prefix, suffix = triangles()
    t2 = jnp.transpose(target, (1, 0, 2)).reshape(FEATS * tiles, PIX)
    t2 = jnp.stack([t2[:, :LANE], t2[:, LANE:]])
    image, grads = pl.pallas_call(
        tiles_kernel,
        out_shape=(
            jax.ShapeDtypeStruct((2, FEATS * tiles, LANE), F32),
            jax.ShapeDtypeStruct((peers * 32, LANE), F32),
        ),
        in_specs=[smem] * 3 + [vmem] * 4,
        out_specs=(vmem, pl.BlockSpec(memory_space=pl.ANY)),
        scratch_shapes=[
            *[pltpu.SMEM((steps + 2 * PAD,), jnp.int32)] * 5,
            *[pltpu.VMEM((peers * 64 + 8, LANE), F32)] * (1 + ACCS),
            pltpu.VMEM((STEP, LANE), F32),
            pltpu.VMEM((STEP, LANE), F32),
            pltpu.VMEM((steps + 4, ROW, STEP), BF16),
            pltpu.VMEM((steps + 4, 16, STEP), F32),
            pltpu.VMEM((RING, PIX, 2 * STEP), BF16),
            pltpu.VMEM((RING, PIX, STEP), F32),
            pltpu.VMEM((PIX, LANE), F32),
            pltpu.VMEM((PIX, LANE), F32),
            pltpu.VMEM((64, PIX), F32),
            pltpu.VMEM((2, FEATS * tiles, LANE), F32),
            pltpu.VMEM((tiles, 2 * ROW, PIX), BF16),
            pltpu.VMEM((tiles, PIX, 2 * ROW), BF16),
            pltpu.VMEM((ROW, STEP), F32),
            pltpu.VMEM((ROW, STEP), BF16),
            pltpu.VMEM((16, STEP), F32),
            pltpu.VMEM((PIX, 2 * STEP), BF16),
            pltpu.VMEM((PIX, STEP), F32),
            pltpu.VMEM((2 * ROW, PIX), BF16),
            pltpu.VMEM((PIX, 2 * ROW), BF16),
            *[pltpu.VMEM((16, STEP), F32)] * 3,
            pltpu.VMEM((STEP, LANE), F32),
            pltpu.VMEM((peers * 32, LANE), F32),
            pltpu.SemaphoreType.DMA,
        ],
        compiler_params=pltpu.CompilerParams(vmem_limit_bytes=52 << 20),
    )(lens, flat, cam, pairs, t2, prefix, suffix)
    image = jnp.concatenate([image[0], image[1]], axis=1).reshape(FEATS, tiles, PIX)
    return jnp.transpose(image, (1, 0, 2)), grads


def serve_kernel(slot_major, table_lo, served):
    peers = slot_major.shape[1]
    lane = lax.broadcasted_iota(jnp.int32, (64, LANE), 1)
    upper = lane // 64
    mat = jnp.transpose(table_lo[...].astype(F32)).astype(BF16)

    def step(g, c):
        ids = pltpu.roll(slot_major[...], lax.rem(peers - g * 32, peers), 1)
        cols = [jnp.broadcast_to(ids[:, k:k + 1], (64, LANE)) for k in range(32)]
        hot = [
            jnp.concatenate(
                [jnp.where((col & 255) == lane + q * LANE, 1.0, 0.0).astype(BF16) for q in range(2)],
                axis=1,
            )
            for col in cols
        ]
        got = dot(jnp.concatenate(hot, axis=0), mat)
        for k in range(32):
            high = (cols[k] >> 8) - upper
            total = jnp.zeros((64, LANE), F32)
            for q in range(4):
                part = got[k * 64:(k + 1) * 64, q * LANE:(q + 1) * LANE]
                total = total + jnp.where(high == 2 * q, part, 0.0)
            total = total + pltpu.roll(total, 64, 1)
            out = jnp.where(lane[:32] < 64, total[:32], total[32:])
            served[pl.ds(pl.multiple_of((g * 32 + k) * 32, 32), 32), :] = out.astype(BF16)
        return c

    lax.fori_loop(0, peers // 32, step, 0)


def serve(incoming, table):
    peers = incoming.shape[0]
    turned = jnp.transpose(table)
    turned = jnp.concatenate([turned[ROW - FEATS:], turned[:ROW - FEATS]], axis=0)
    turned = turned.reshape(ROW, 8, PIX).transpose(1, 0, 2).reshape(8 * ROW, PIX)
    vmem = pl.BlockSpec(memory_space=pltpu.VMEM)
    return pl.pallas_call(
        serve_kernel,
        out_shape=jax.ShapeDtypeStruct((peers * 32, LANE), BF16),
        in_specs=[vmem, vmem],
        out_specs=vmem,
        compiler_params=pltpu.CompilerParams(vmem_limit_bytes=32 << 20),
    )(jnp.transpose(incoming), turned)


def collect_kernel(slot_major, flat, pairs, owned, total):
    peers = slot_major.shape[1]
    lane = lax.broadcasted_iota(jnp.int32, (64, LANE), 1)
    upper = lane // 64
    left = lane[:32] < 64
    low_id = lax.broadcasted_iota(jnp.int32, (512, LANE), 0)
    total[...] = jnp.zeros_like(total)

    def step(g, c):
        ids = pltpu.roll(slot_major[...], lax.rem(peers - g * 32, peers), 1)
        hot = []
        for k in range(16):
            row = flat[pl.ds(g * 16 + k, 1), :] & 511
            hot.append(jnp.where(low_id == row, 1.0, 0.0).astype(BF16))
        blocks = []
        for k in range(32):
            high = (jnp.broadcast_to(ids[:, k:k + 1], (64, LANE)) >> 9) - upper
            two = pairs[pl.ds(pl.multiple_of((g * 32 + k) * 32, 32), 32), :]
            other = pltpu.roll(two, 64, 1)
            both = jnp.concatenate(
                [jnp.where(left, two, other), jnp.where(left, other, two)], axis=0
            )
            hi = both.astype(BF16).astype(F32)
            parts = [
                jnp.where(high == 2 * q, part, 0.0).astype(BF16)
                for part in (hi, both - hi)
                for q in range(2)
            ]
            blocks.append(jnp.concatenate(parts, axis=1))
        total[...] += dot(jnp.concatenate(hot, axis=1), jnp.concatenate(blocks, axis=0))
        return c

    lax.fori_loop(0, peers // 32, step, 0)
    whole = jnp.transpose(total[:, :256] + total[:, 256:])
    for q in range(4):
        part = whole[q * 64:(q + 1) * 64]
        owned[:, q * 512:(q + 1) * 512] = jnp.concatenate([part[FEATS:], part[:FEATS]], axis=0)


def collect(incoming, pairs, rows):
    peers = incoming.shape[0]
    vmem = pl.BlockSpec(memory_space=pltpu.VMEM)
    owned = pl.pallas_call(
        collect_kernel,
        out_shape=jax.ShapeDtypeStruct((ROW, rows), F32),
        in_specs=[vmem] * 3,
        out_specs=vmem,
        scratch_shapes=[pltpu.VMEM((512, 512), F32)],
        compiler_params=pltpu.CompilerParams(vmem_limit_bytes=32 << 20),
    )(jnp.transpose(incoming), incoming.reshape(-1, LANE), pairs)
    return jnp.transpose(owned)


def exchange(x):
    return lax.all_to_all(x, ("gauss", "view"), split_axis=0, concat_axis=0, tiled=True)


def shards(table, view_proj, lengths, lists, requests, target):
    incoming = exchange(requests[0, 0])
    peers = incoming.shape[0]
    served = serve(incoming, table)
    pairs = exchange(served.reshape(peers, 32, LANE)).reshape(peers * 32, LANE)
    image, grads = render(lengths[0], lists[0], view_proj[0], pairs, target[0])
    returned = exchange(grads.reshape(peers, 32, LANE)).reshape(peers * 32, LANE)
    return image[None], collect(incoming, returned, table.shape[0])


def solution(mesh):
    return jax.shard_map(
        shards,
        mesh=mesh,
        in_specs=(
            P(("gauss", "view"), None),
            P("view", None, None),
            P("view", "gauss"),
            P("view", "gauss", None),
            P("view", "gauss", None, None),
            P("view", "gauss", None, None),
        ),
        out_specs=(P("view", "gauss", None, None), P(("gauss", "view"), None)),
        check_vma=False,
    )
```

```python
import functools

import functools

import jax
import jax.numpy as jnp
from jax import lax
from jax.experimental import pallas as pl
from jax.experimental.pallas import tpu as pltpu
from jax.sharding import PartitionSpec as P

LOG2E = 1.4426950408889634
FEATS = 57
ROW = 64
LANE = 128
PIX = 256
ACCS = 4
STEP = 256
RING = 9
PAD = 16
ORDER = "fbfbfbffbb"
ONE = ""
DRIP = 6
F32 = jnp.float32
BF16 = jnp.bfloat16


def split(x):
    hi = x.astype(BF16)
    lo = (x - hi.astype(F32)).astype(BF16)
    return hi, lo


def dot(a, b):
    return jnp.dot(a, b, preferred_element_type=F32)


def dot_t(a, b):
    return lax.dot_general(a, b, (((1,), (1,)), ((), ())), preferred_element_type=F32)


def unpack_rows(pairs_ref, rows_ref, peers):
    def step(i, c):
        for k in range(8):
            o = i * 8 + k
            two = pairs_ref[pl.ds(pl.multiple_of(o * 32, 32), 32), :].astype(F32)
            base = pl.multiple_of(o * 64, 64)
            rows_ref[pl.ds(base, 32), :] = two
            rows_ref[pl.ds(pl.multiple_of(base + 32, 32), 32), :] = pltpu.roll(two, 64, 1)
        return c

    lax.fori_loop(0, peers // 8, step, 0)


def pack_rows(accs, pairs_ref, out_ref, sem, peers):
    lane = lax.broadcasted_iota(jnp.int32, (32, LANE), 1)

    def step(i, c):
        for k in range(8):
            o = i * 8 + k
            base = pl.multiple_of(o * 64, 64)
            first = sum(acc[pl.ds(base, 32), :] for acc in accs)
            second = sum(acc[pl.ds(pl.multiple_of(base + 32, 32), 32), :] for acc in accs)
            pairs_ref[pl.ds(pl.multiple_of(o * 32, 32), 32), :] = jnp.where(
                lane < 64, first, pltpu.roll(second, 64, 1)
            )
        part = pl.ds(pl.multiple_of(i * 256, 256), 256)
        pltpu.make_async_copy(pairs_ref.at[part], out_ref.at[part], sem).start()
        return c

    lax.fori_loop(0, peers // 8, step, 0)
    pltpu.make_async_copy(pairs_ref, out_ref, sem).wait()


def tiles_kernel(
    lens, lists, cam,
    pairs, target, prefix_mat, suffix_mat,
    image, out_pairs,
    base_of, tile_of, first_of, mirror_of, live_of,
    rows, acc0, acc1, acc2, acc3,
    splats, grows, feat_t, geo, weights, ratio, entering_ref, later_ref, pic, tgt, pull_rows, pull_t, grow_t,
    feat_new, geo_new, weights_new, ratio_new, rows_new, cols_new,
    dy_back, dy_front, qc_front, splats_new, packed, sem,
):
    accs = (acc0, acc1, acc2, acc3)
    tiles = lens.shape[0]
    peers = pairs.shape[0] // 32
    entries = lists.shape[0] // (tiles + 1)

    def blank(i, c):
        base_of[i] = tiles * entries
        tile_of[i] = 0
        first_of[i] = 1
        mirror_of[i] = 0
        live_of[i] = 0
        return c

    lax.fori_loop(0, base_of.shape[0], blank, 0)

    def list_tile(t, at):
        steps = (lens[t] + STEP - 1) // STEP

        def list_step(j, c):
            where = at + j + PAD
            base_of[where] = t * entries + j * STEP
            tile_of[where] = t
            first_of[where] = jnp.where(j == 0, 1, 0)
            mirror_of[where] = at + steps - 1 - j
            live_of[where] = lens[t] - j * STEP
            return c

        lax.fori_loop(0, steps, list_step, 0)
        return at + steps

    count = lax.fori_loop(0, tiles, list_tile, 0)

    unpack_rows(pairs, rows, peers)
    rows[peers * 64:, :] = jnp.zeros((8, LANE), F32)

    def clear(i, c):
        for acc in accs:
            acc[pl.ds(pl.multiple_of(i * 64, 64), 64), :] = jnp.zeros((64, LANE), F32)
        return c

    lax.fori_loop(0, peers, clear, 0)
    tgt[...] = target[...].astype(F32)
    splats_new[...] = jnp.zeros_like(splats_new)
    feat_new[...] = jnp.zeros_like(feat_new)
    geo_new[...] = jnp.zeros_like(geo_new)

    prefix = prefix_mat[...]
    suffix = suffix_mat[...]
    sub16 = lax.broadcasted_iota(jnp.int32, (16, STEP), 0).astype(F32) + 0.5
    lane256 = lax.broadcasted_iota(jnp.int32, (1, STEP), 1)
    feature = lax.broadcasted_iota(jnp.int32, (64, PIX), 0) < FEATS

    def scatter(s):
        base = base_of[mirror_of[s + PAD] + PAD]
        base = jnp.where(live_of[s + PAD] > 0, base, tiles * entries)

        def rows_from(q):
            ids = [lists[base + q + k] for k in range(ACCS)]
            old = [accs[k][pl.ds(ids[k], 1), :] for k in range(ACCS)]
            for k in range(ACCS):
                accs[k][pl.ds(ids[k], 1), :] = old[k] + grows[q + k:q + k + 1, :]

        return [functools.partial(rows_from, q) for q in range(0, STEP, ACCS)]

    def turn_back():
        for k in range(2):
            part = jnp.concatenate(
                [grow_t[:, k * LANE:(k + 1) * LANE], jnp.zeros((64, LANE), F32)], axis=0
            )
            grows[k * LANE:(k + 1) * LANE, :] = jnp.transpose(part)

    def coords(g):
        return sub16 - geo[g, 0:1, :], sub16 - geo[g, 1:2, :]

    def spread(ref, cut):
        return jnp.stack([jnp.broadcast_to(ref[y:y + 1, cut], (16, LANE)) for y in range(16)])

    def backward(b, drip):
        f = mirror_of[b + PAD]
        g = f + 2
        slot = lax.rem(g, RING)
        t = tile_of[b + PAD]
        keep = first_of[b + PAD] == 0
        dx, dy = coords(g)
        dy_back[...] = dy
        ft = feat_t[g]
        halves = weights[slot]
        d_weight = dot(pull_t[t], jnp.concatenate([ft, ft], axis=0))
        quads = dot(pull_rows[t], halves)
        quads = quads[:64] + quads[64:]
        yield
        prods, boths, sums = [None, None], [None, None], [None, None]
        for k in (1, 0):
            cut = slice(k * LANE, (k + 1) * LANE)
            weight = (
                halves[:, 2 * k * LANE:(2 * k + 1) * LANE].astype(F32)
                + halves[:, (2 * k + 1) * LANE:(2 * k + 2) * LANE].astype(F32)
            )
            prods[k] = weight * d_weight[:, cut]
            drip()
            boths[k] = dot(jnp.concatenate(split(prods[k]), axis=1), suffix)
            drip()
            yield
        later = jnp.where(keep, later_ref[...], 0.0)
        for k in (1, 0):
            cut = slice(k * LANE, (k + 1) * LANE)
            h = prods[k] - ratio[slot, :, cut] * (boths[k][:, :LANE] + later)
            drip()
            later = later + boths[k][:, LANE:]
            drip()
            h = h.reshape(16, 16, LANE)
            dyk = spread(dy_back, cut)
            hy = h * dyk
            drip()
            sums[k] = (
                jnp.sum(h, axis=0),
                jnp.sum(hy, axis=0),
                jnp.sum(hy * dyk, axis=0),
            )
            yield
        later_ref[...] = later
        s0, s1, s2 = (jnp.concatenate([sums[0][j], sums[1][j]], axis=1) for j in range(3))
        sx = s0 * dx
        m0, mx, my, mxx, mxy, myy = (
            jnp.sum(m, axis=0, keepdims=True) for m in (s0, sx, s1, sx * dx, s1 * dx, s2)
        )
        ca, cb, cc = geo[g, 6:7, :], geo[g, 7:8, :], geo[g, 8:9, :]
        du = (ca * mx + cb * my) * geo[g, 9:10, :]
        dw = (cb * mx + cc * my) * geo[g, 10:11, :]
        shared = -0.5 * cb * mxy
        first = jnp.concatenate(
            [quads[:, 0:LANE] + quads[:, LANE:2 * LANE],
             quads[:, 2 * LANE:3 * LANE] + quads[:, 3 * LANE:]], axis=1
        )
        grow_t[0:56, :] = first[0:56]
        grow_t[56:57, :] = first[56:57]
        outs = (
            du * cam[0, 0] + dw * cam[1, 0],
            du * cam[0, 1] + dw * cam[1, 1],
            du * cam[0, 2] + dw * cam[1, 2],
            -0.5 * ca * mxx + shared,
            -0.5 * cc * myy + shared,
            -mxy * geo[g, 11:12, :],
            geo[g, 12:13, :] * m0,
        )
        for j, value in enumerate(outs):
            grow_t[57 + j:58 + j, :] = value

    def pull(p):
        t = tile_of[p + PAD]
        picture = pic[...]
        for h in range(2):
            image[h, pl.ds(t, FEATS, stride=tiles), :] = picture[:FEATS, h * LANE:(h + 1) * LANE]
        want = jnp.concatenate(
            [tgt[h, pl.ds(t, FEATS, stride=tiles), :] for h in range(2)], axis=1
        )
        want = jnp.concatenate([want, jnp.zeros((64 - FEATS, PIX), F32)], axis=0)
        diff = jnp.where(feature, picture - want, 0.0)
        hi, lo = split(diff)
        both = jnp.concatenate([hi, lo], axis=0)
        rows_new[...] = both
        cols_new[...] = jnp.transpose(both.astype(F32)).astype(BF16)

    def forward(f, drip):
        g = f + 2
        keep = first_of[f + PAD] == 0
        dx, dy = coords(g)
        qa = geo[g, 2:3, :] * dx * dx
        qb = geo[g, 3:4, :] * dx
        qc = geo[g, 4:5, :] * dy * dy + geo[g, 5:6, :]
        dy_front[...] = dy
        qc_front[...] = qc
        entering = jnp.where(keep, entering_ref[...], 0.0)
        parts, kept = [], []
        for k in range(2):
            cut = slice(k * LANE, (k + 1) * LANE)
            power = qa[None, :, cut] + qb[None, :, cut] * spread(dy_front, cut) + spread(qc_front, cut)
            alpha = jnp.exp2(power.reshape(PIX, LANE))
            drip()
            rest = 1.0 - alpha
            logs = jnp.log2(rest)
            drip()
            both = dot(jnp.concatenate(split(logs), axis=1), prefix)
            ratio_new[:, cut] = alpha * pl.reciprocal(rest, approx=True)
            drip()
            kept.append((alpha, both))
            yield
        for alpha, both in kept:
            weight = alpha * jnp.exp2(both[:, :LANE] + entering)
            drip()
            entering = entering + both[:, LANE:]
            parts.extend(split(weight))
            drip()
            yield
        entering_ref[...] = entering
        halves = jnp.concatenate(parts, axis=1)
        weights_new[...] = halves
        ft = feat_t[g]
        left, right = ft[:, :LANE], ft[:, LANE:]
        pic[...] = jnp.where(keep, pic[...], 0.0) + dot_t(
            jnp.concatenate([left, left, right, right], axis=1), halves
        )

    def prepare(x):
        turned = [
            jnp.transpose(splats[k * LANE:(k + 1) * LANE, :])[0:64] for k in range(2)
        ]
        turned = jnp.concatenate(turned, axis=1)
        feat_new[...] = turned.astype(BF16)
        px, py, pz, sa, sc, sb, so = (turned[57 + j:58 + j, :] for j in range(7))
        tu = jnp.tanh(px * cam[0, 0] + py * cam[0, 1] + pz * cam[0, 2] + cam[0, 3])
        tw = jnp.tanh(px * cam[1, 0] + py * cam[1, 1] + pz * cam[1, 2] + cam[1, 3])
        ca, cc = jnp.exp(sa), jnp.exp(sc)
        tb = jnp.tanh(sb)
        root = 0.9 * jnp.sqrt(ca * cc)
        cb = tb * root
        soft = jnp.exp(-jnp.abs(so))
        log_o = jnp.minimum(so, 0.0) * LOG2E - jnp.log2(1.0 + soft)
        half = -0.5 * LOG2E
        values = (
            8.0 + 6.0 * tu,
            8.0 + 6.0 * tw,
            half * ca,
            (2.0 * half) * cb,
            half * cc,
            jnp.where(lane256 < live_of[x + PAD], log_o, -1e30),
            ca,
            cb,
            cc,
            6.0 * (1.0 - tu * tu),
            6.0 * (1.0 - tw * tw),
            root * (1.0 - tb * tb),
            jnp.where(so >= 0.0, soft, 1.0) / (1.0 + soft),
        )
        for j, value in enumerate(values):
            geo_new[j:j + 1, :] = value

    def gather(n):
        base = base_of[n + PAD]

        def rows_from(q):
            got = [rows[pl.ds(lists[base + q + j], 1), :] for j in range(4)]
            for j in range(4):
                splats_new[q + j:q + j + 1, :] = got[j]

        return [functools.partial(rows_from, q) for q in range(0, STEP, 4)]

    def file(n):
        feat_t[n] = feat_new[...]
        geo[n] = geo_new[...]
        slot = lax.rem(n + RING - 1, RING)
        weights[slot] = weights_new[...]
        ratio[slot] = ratio_new[...]
        t = tile_of[n - 4 + PAD]
        pull_rows[t] = rows_new[...]
        pull_t[t] = cols_new[...]

    moves = []

    def drip(share=1.0):
        for _ in range(min(len(moves), max(1, int(DRIP * share)))):
            moves.pop(0)()

    def flush():
        while moves:
            moves.pop(0)()

    def run(order, front, back):
        for letter in order:
            stage = front if letter == "f" else back
            if stage is not None:
                next(stage, None)
        for stage in (front, back):
            if stage is not None:
                for _ in stage:
                    pass

    def opening(n, c):
        splats[...] = splats_new[...]
        file(n)
        pull(n - 3)
        prepare(n - 1)
        moves.extend(gather(n))
        run(ONE, forward(n - 2, drip), None)
        flush()
        return c

    def middle(n, c):
        @pl.when(n > 0)
        def _():
            splats[...] = splats_new[...]

        file(n)
        turn_back()

        prepare(n - 1)
        pull(n - 3)
        for pair in zip(scatter(n - 8), gather(n)):
            moves.extend(pair)
        run(ORDER, forward(n - 2, drip), backward(n - 7, drip))
        flush()
        return c

    def closing(n, c):
        turn_back()
        moves.extend(scatter(n - 8))
        run(ONE, None, backward(n - 7, drip))
        flush()
        return c

    moves.extend(gather(0))
    flush()
    splats[...] = splats_new[...]
    prepare(0)
    moves.extend(gather(1))
    flush()
    lax.fori_loop(2, 7, opening, 0)
    lax.fori_loop(7, count + 3, middle, 0)
    file(count + 3)
    lax.fori_loop(count + 3, count + 7, closing, 0)
    turn_back()
    moves.extend(scatter(count - 1))
    flush()
    pack_rows(accs, packed, out_pairs, sem, peers)


def triangles():
    r = lax.broadcasted_iota(jnp.int32, (PIX, PIX), 0) % LANE
    c = lax.broadcasted_iota(jnp.int32, (PIX, PIX), 1)
    prefix = (c >= LANE) | (r < c)
    suffix = (c >= LANE) | (r > c)
    return prefix.astype(BF16), suffix.astype(BF16)


def render(lens, lists, cam, pairs, target):
    tiles, entries = lists.shape
    peers = pairs.shape[0] // 32
    steps = tiles * (entries // STEP)
    live = lax.broadcasted_iota(jnp.int32, lists.shape, 1) < lens[:, None]
    flat = jnp.where(live, lists, peers * 64).reshape(-1)
    flat = jnp.concatenate([flat, jnp.full((entries,), peers * 64, jnp.int32)])
    smem = pl.BlockSpec(memory_space=pltpu.SMEM)
    vmem = pl.BlockSpec(memory_space=pltpu.VMEM)
    prefix, suffix = triangles()
    t2 = jnp.transpose(target, (1, 0, 2)).reshape(FEATS * tiles, PIX)
    t2 = jnp.stack([t2[:, :LANE], t2[:, LANE:]])
    image, grads = pl.pallas_call(
        tiles_kernel,
        out_shape=(
            jax.ShapeDtypeStruct((2, FEATS * tiles, LANE), F32),
            jax.ShapeDtypeStruct((peers * 32, LANE), F32),
        ),
        in_specs=[smem] * 3 + [vmem] * 4,
        out_specs=(vmem, pl.BlockSpec(memory_space=pl.ANY)),
        scratch_shapes=[
            *[pltpu.SMEM((steps + 2 * PAD,), jnp.int32)] * 5,
            *[pltpu.VMEM((peers * 64 + 8, LANE), F32)] * (1 + ACCS),
            pltpu.VMEM((STEP, LANE), F32),
            pltpu.VMEM((STEP, LANE), F32),
            pltpu.VMEM((steps + 4, ROW, STEP), BF16),
            pltpu.VMEM((steps + 4, 16, STEP), F32),
            pltpu.VMEM((RING, PIX, 2 * STEP), BF16),
            pltpu.VMEM((RING, PIX, STEP), F32),
            pltpu.VMEM((PIX, LANE), F32),
            pltpu.VMEM((PIX, LANE), F32),
            pltpu.VMEM((64, PIX), F32),
            pltpu.VMEM((2, FEATS * tiles, LANE), F32),
            pltpu.VMEM((tiles, 2 * ROW, PIX), BF16),
            pltpu.VMEM((tiles, PIX, 2 * ROW), BF16),
            pltpu.VMEM((ROW, STEP), F32),
            pltpu.VMEM((ROW, STEP), BF16),
            pltpu.VMEM((16, STEP), F32),
            pltpu.VMEM((PIX, 2 * STEP), BF16),
            pltpu.VMEM((PIX, STEP), F32),
            pltpu.VMEM((2 * ROW, PIX), BF16),
            pltpu.VMEM((PIX, 2 * ROW), BF16),
            *[pltpu.VMEM((16, STEP), F32)] * 3,
            pltpu.VMEM((STEP, LANE), F32),
            pltpu.VMEM((peers * 32, LANE), F32),
            pltpu.SemaphoreType.DMA,
        ],
        compiler_params=pltpu.CompilerParams(vmem_limit_bytes=202 << 18),
    )(lens, flat, cam, pairs, t2, prefix, suffix)
    image = jnp.concatenate([image[0], image[1]], axis=1).reshape(FEATS, tiles, PIX)
    return jnp.transpose(image, (1, 0, 2)), grads


def serve_kernel(slot_major, table_lo, served):
    peers = slot_major.shape[1]
    lane = lax.broadcasted_iota(jnp.int32, (64, LANE), 1)
    upper = lane // 64
    mat = jnp.transpose(table_lo[...].astype(F32)).astype(BF16)

    def step(g, c):
        ids = pltpu.roll(slot_major[...], lax.rem(peers - g * 32, peers), 1)
        cols = [jnp.broadcast_to(ids[:, k:k + 1], (64, LANE)) for k in range(32)]
        hot = [
            jnp.concatenate(
                [jnp.where((col & 255) == lane + q * LANE, 1.0, 0.0).astype(BF16) for q in range(2)],
                axis=1,
            )
            for col in cols
        ]
        got = dot(jnp.concatenate(hot, axis=0), mat)
        for k in range(32):
            high = (cols[k] >> 8) - upper
            total = jnp.zeros((64, LANE), F32)
            for q in range(4):
                part = got[k * 64:(k + 1) * 64, q * LANE:(q + 1) * LANE]
                total = total + jnp.where(high == 2 * q, part, 0.0)
            total = total + pltpu.roll(total, 64, 1)
            out = jnp.where(lane[:32] < 64, total[:32], total[32:])
            served[pl.ds(pl.multiple_of((g * 32 + k) * 32, 32), 32), :] = out.astype(BF16)
        return c

    lax.fori_loop(0, peers // 32, step, 0)


def serve(incoming, table):
    peers = incoming.shape[0]
    turned = jnp.transpose(table)
    turned = jnp.concatenate([turned[ROW - FEATS:], turned[:ROW - FEATS]], axis=0)
    turned = turned.reshape(ROW, 8, PIX).transpose(1, 0, 2).reshape(8 * ROW, PIX)
    vmem = pl.BlockSpec(memory_space=pltpu.VMEM)
    return pl.pallas_call(
        serve_kernel,
        out_shape=jax.ShapeDtypeStruct((peers * 32, LANE), BF16),
        in_specs=[vmem, vmem],
        out_specs=vmem,
        compiler_params=pltpu.CompilerParams(vmem_limit_bytes=32 << 20),
    )(jnp.transpose(incoming), turned)


def collect_kernel(slot_major, flat, pairs, owned, total):
    peers = slot_major.shape[1]
    lane = lax.broadcasted_iota(jnp.int32, (64, LANE), 1)
    upper = lane // 64
    left = lane[:32] < 64
    low_id = lax.broadcasted_iota(jnp.int32, (512, LANE), 0)
    total[...] = jnp.zeros_like(total)

    def step(g, c):
        ids = pltpu.roll(slot_major[...], lax.rem(peers - g * 32, peers), 1)
        hot = []
        for k in range(16):
            row = flat[pl.ds(g * 16 + k, 1), :] & 511
            hot.append(jnp.where(low_id == row, 1.0, 0.0).astype(BF16))
        blocks = []
        for k in range(32):
            high = (jnp.broadcast_to(ids[:, k:k + 1], (64, LANE)) >> 9) - upper
            two = pairs[pl.ds(pl.multiple_of((g * 32 + k) * 32, 32), 32), :]
            other = pltpu.roll(two, 64, 1)
            both = jnp.concatenate(
                [jnp.where(left, two, other), jnp.where(left, other, two)], axis=0
            )
            hi = both.astype(BF16).astype(F32)
            parts = [
                jnp.where(high == 2 * q, part, 0.0).astype(BF16)
                for part in (hi, both - hi)
                for q in range(2)
            ]
            blocks.append(jnp.concatenate(parts, axis=1))
        total[...] += dot(jnp.concatenate(hot, axis=1), jnp.concatenate(blocks, axis=0))
        return c

    lax.fori_loop(0, peers // 32, step, 0)
    whole = jnp.transpose(total[:, :256] + total[:, 256:])
    for q in range(4):
        part = whole[q * 64:(q + 1) * 64]
        owned[:, q * 512:(q + 1) * 512] = jnp.concatenate([part[FEATS:], part[:FEATS]], axis=0)


def collect(incoming, pairs, rows):
    peers = incoming.shape[0]
    vmem = pl.BlockSpec(memory_space=pltpu.VMEM)
    owned = pl.pallas_call(
        collect_kernel,
        out_shape=jax.ShapeDtypeStruct((ROW, rows), F32),
        in_specs=[vmem] * 3,
        out_specs=vmem,
        scratch_shapes=[pltpu.VMEM((512, 512), F32)],
        compiler_params=pltpu.CompilerParams(vmem_limit_bytes=32 << 20),
    )(jnp.transpose(incoming), incoming.reshape(-1, LANE), pairs)
    return jnp.transpose(owned)


def exchange(x):
    return lax.all_to_all(x, ("gauss", "view"), split_axis=0, concat_axis=0, tiled=True)


def shards(table, view_proj, lengths, lists, requests, target):
    incoming = exchange(requests[0, 0])
    peers = incoming.shape[0]
    served = serve(incoming, table)
    pairs = exchange(served.reshape(peers, 32, LANE)).reshape(peers * 32, LANE)
    image, grads = render(lengths[0], lists[0], view_proj[0], pairs, target[0])
    returned = exchange(grads.reshape(peers, 32, LANE)).reshape(peers * 32, LANE)
    return image[None], collect(incoming, returned, table.shape[0])


def solution(mesh):
    return jax.shard_map(
        shards,
        mesh=mesh,
        in_specs=(
            P(("gauss", "view"), None),
            P("view", None, None),
            P("view", "gauss"),
            P("view", "gauss", None),
            P("view", "gauss", None, None),
            P("view", "gauss", None, None),
        ),
        out_specs=(P("view", "gauss", None, None), P(("gauss", "view"), None)),
        check_vma=False,
    )
```
